512 devices in a mesh: dp: 32 (over x, z_lo, core), mp: 16 (over y, z_hi).
Axes of the slice: x: 4, y: 8, z: 8 (z_hi: 2, z_lo: 4; z = z_hi * 4 + z_lo), core: 2. Of those that a mesh axis runs over, the one named last changes fastest.
Arguments:
- sig_feat: bfloat16 [256, 64, 1152], P('dp', None, 'mp'), may hold values from -6 to 6
- conv_feat: bfloat16 [256, 64, 3072], P('dp', None, 'mp'), may hold values from -6 to 6
- proj_weight: bfloat16 [4224, 7168], P('dp', 'mp'), may hold values from -0.09375 to 0.09375
- norm_gain: float32 [7168], P('mp'), may hold values from 0.5 to 1.5
- text_embed: bfloat16 [16384, 7168], P('dp', 'mp'), may hold values from -6 to 6
- grad_out: bfloat16 [16384, 7168], P('dp', 'mp'), may hold values from -6 to 6
- tile_count: int32 [32], P('dp'), may hold values from 1 to 8, 144 in all
- tile_block: int32 [32, 8], P('dp'), may hold values from 0 to 7, each once within a row
Outputs:
- normed: bfloat16 [16384, 7168], P('dp', 'mp')
- grad_sig: bfloat16 [256, 64, 1152], P('dp', None, 'mp')
- grad_conv: bfloat16 [256, 64, 3072], P('dp', None, 'mp')
The draws below stay inside these ranges and needn't reach their ends.
Inputs may be any that keep to these rules, and one draw needn't show every extreme that they name: `tile_block`: each row holds every block number of a shard once.
All inputs are finite; a program needn't handle non-finite values. No bound on the sum of `tile_count` on one device may be relied on, other than what follows from the above.
Results may differ from the reference program's by a relative error of at most 0.019.
Values may be sent and summed in bfloat16 or wider, within the bound.
No kernel may reach another device: no remote copies, remote signals or barrier semaphores. Data moves between devices by JAX's collectives and lax.ppermute only.
A program may use at most 64 MiB of HBM per device.

```python
import math
import jax
import jax.numpy as jnp
import numpy as np
from jax import lax

D = 7168
CS = 1152
CC = 3072
TT = 64
TCAP = 8
S_DEV = 512
TILES = 256
S_TOT = 16384
N_DP = 32
N_MP = 16


def shard_levels(own_key, extent, cuts, least, largest):
    level, own = 1.0, jax.random.fold_in(own_key, 6)
    for position, blocks in cuts:
        steps = jnp.exp(jax.random.uniform(jax.random.fold_in(own, position), (blocks,), jnp.float32, least / len(cuts), largest / len(cuts)))
        level = level * jnp.repeat(steps, extent[position] // blocks).reshape([-1 if axis == position else 1 for axis in range(len(extent))])
    return level


def profile(number_of, total, most, slope):
    portions = [(1 << 20) // math.isqrt(standing ** slope) + 1 for standing in range(2, number_of + 1)]
    spare, given = total - most - (number_of - 1), [1] * (number_of - 1)
    while spare > 0:
        candidates = [i for i in range(number_of - 1) if given[i] < most]
        mass, left = sum([portions[i] for i in candidates]), spare
        for i in candidates:
            more = min(most - given[i], max(1, left * portions[i] // mass), spare)
            given[i] = given[i] + more
            spare = spare - more
    return np.array([most] + given)


def ragged(stream_key, amount, total, bound, lean):
    if amount == 2:
        one = jax.random.randint(stream_key, (), max(1, total - bound), min(bound, total - 1) + 1)
        return jnp.stack([one, total - one])
    lengths = jnp.asarray(profile(amount, total, bound, lean), jnp.int32)
    couples = (amount - 1) // 2
    source_of, sink = lengths[1:1 + 2 * couples:2], lengths[2:2 + 2 * couples:2]
    margin = jnp.minimum(source_of - 1, bound - sink)
    moved = jax.random.randint(jax.random.fold_in(stream_key, 1), (couples,), 0, 1 << 20) % (margin + 1)
    lengths = lengths.at[1:1 + 2 * couples:2].set(source_of - moved).at[2:2 + 2 * couples:2].set(sink + moved)
    return lengths[jax.random.permutation(jax.random.fold_in(stream_key, 2), amount)]


def gaussian(rng, extent, scale, reach, shards=(), kind=jnp.bfloat16):
    loudness = shard_levels(rng, extent, shards, -0.22, 0.18) if shards else 1.0
    values = jax.random.normal(rng, extent, jnp.float32) * scale * loudness
    return jnp.minimum(jnp.maximum(values, -reach), reach).astype(kind)


def setup_inputs(seed: int = 0) -> dict:
    arg_keys = jax.random.split(jax.random.key(seed), 9)
    return {
        "sig_feat": gaussian(arg_keys[0], (TILES, TT, CS), 1.0, 6.0, ((0, 32), (2, 16))),
        "conv_feat": gaussian(arg_keys[1], (TILES, TT, CC), 1.0, 6.0, ((0, 32), (2, 16))),
        "proj_weight": gaussian(arg_keys[2], (CS + CC, D), (CS + CC) ** -0.5, 0.09375, ((0, 32), (1, 16))),
        "norm_gain": jnp.clip(1.0 + 0.1 * jax.random.normal(arg_keys[3], (D,), jnp.float32), 0.5, 1.5),
        "text_embed": gaussian(arg_keys[4], (S_TOT, D), 1.0, 6.0, ((0, 32), (1, 16))),
        "grad_out": gaussian(arg_keys[5], (S_TOT, D), 1.0, 6.0, ((0, 32), (1, 16))),
        "tile_count": ragged(arg_keys[6], N_DP, N_DP + N_DP * (TCAP - 1) // 2, TCAP, 2).astype(jnp.int32),
        "tile_block": jax.vmap(lambda own: jax.random.permutation(own, S_DEV // TT))(jax.random.split(arg_keys[7], N_DP)).reshape((N_DP, S_DEV // TT)).astype(jnp.int32),
    }


def gelu_tanh(value):
    return jax.nn.gelu(value, approximate=True)

def reference(sig_feat, conv_feat, proj_weight, norm_gain, text_embed, grad_out, tile_count, tile_block):
    n_data = N_DP
    n_blocks = S_DEV // TT
    tile_rows = TCAP * TT
    conv_home = jnp.roll(conv_feat.reshape(n_data, TCAP, TT, CC), -(n_data // 2), axis=0)
    sig_rows = sig_feat.reshape(n_data, tile_rows, CS)
    conv_rows = conv_home.reshape(n_data, tile_rows, CC)
    live_tile = jnp.arange(TCAP, dtype=jnp.int32)[None, :] < tile_count[:, None]
    block_of = tile_block[:, :TCAP]
    chooser = ((block_of[:, None, :] == jnp.arange(n_blocks, dtype=jnp.int32)[None, :, None]) & live_tile[:, None, :]).astype(jnp.float32)
    embeds = text_embed.reshape(n_data, S_DEV, D)
    cotangent = grad_out.reshape(n_data, S_DEV, D)
    w_sig = proj_weight[:CS]
    w_conv = proj_weight[CS:]
    gain = norm_gain.astype(jnp.float32)
    width_mp = D // N_MP
    weight_groups = proj_weight.astype(jnp.float32).reshape(CS + CC, N_MP, width_mp)

    def per_shard(pieces):
        sig_part, conv_part, embed_part, cot_part, choose = pieces
        pre_act = jnp.dot(sig_part, w_sig, preferred_element_type=jnp.float32) + jnp.dot(conv_part, w_conv, preferred_element_type=jnp.float32)
        image = gelu_tanh(pre_act).astype(jnp.bfloat16)
        placed = jnp.einsum('bi,itd->btd', choose, image.reshape(TCAP, TT, D).astype(jnp.float32), precision=lax.Precision.HIGHEST)
        is_image = lax.optimization_barrier(jnp.sum(choose, axis=1)) > 0
        mixed = jnp.where(is_image[:, None, None], placed, embed_part.reshape(n_blocks, TT, D).astype(jnp.float32)).astype(jnp.bfloat16)
        embed_f = mixed.reshape(S_DEV, D).astype(jnp.float32)
        inv_rms = lax.rsqrt(lax.optimization_barrier(jnp.mean(embed_f * embed_f, axis=1)) + 1e-05)
        normed = (embed_f * inv_rms[:, None] * gain[None, :]).astype(jnp.bfloat16)
        scaled_cot = cot_part.astype(jnp.float32) * gain[None, :]
        back_dot = lax.optimization_barrier(jnp.sum(scaled_cot * embed_f, axis=1))
        grad_mixed = inv_rms[:, None] * scaled_cot - embed_f * (inv_rms ** 3 * back_dot / D)[:, None]
        grad_image = jnp.einsum('bi,btd->itd', choose, grad_mixed.reshape(n_blocks, TT, D), precision=lax.Precision.HIGHEST).reshape(tile_rows, D)
        unused, pull_back = jax.vjp(gelu_tanh, pre_act)
        grad_pre = pull_back(grad_image)[0].astype(jnp.bfloat16)
        grad_groups = grad_pre.astype(jnp.float32).reshape(tile_rows, N_MP, width_mp)
        partials = jnp.einsum('tmk,cmk->mtc', grad_groups, weight_groups, precision=lax.Precision.HIGHEST)
        partials = lax.optimization_barrier(partials.astype(jnp.bfloat16))
        feature_grad = lax.optimization_barrier(jnp.sum(partials.astype(jnp.float32), axis=0)).astype(jnp.bfloat16)
        return (normed, feature_grad[:, :CS], feature_grad[:, CS:])
    normed, grad_sig, grad_conv = lax.map(per_shard, (sig_rows, conv_rows, embeds, cotangent, chooser))
    grad_conv = jnp.roll(grad_conv.reshape(n_data, TCAP, TT, CC), n_data // 2, axis=0)
    return (normed.reshape(S_TOT, D), grad_sig.reshape(TILES, TT, CS), grad_conv.reshape(TILES, TT, CC))
```

```python
import functools
import math

import jax
import jax.numpy as jnp
from jax import lax
from jax.experimental import pallas as pl
from jax.experimental.pallas import tpu as pltpu
from jax.sharding import Mesh
from jax.sharding import PartitionSpec as P

BF = jnp.bfloat16
F32 = jnp.float32
EPS = 1e-05
GELU_K = 0.7978845608
GELU_C = 0.044715

AXES = ("x", "zl", "core", "y", "zh")
ROWS = 132
ROWS_PAD = 136
COLS = 448
COLS_PAD = 512
HALF = 256
SIG = 72
CONV = 192


def shift(x, axis, by):
    n = lax.axis_size(axis)
    return lax.ppermute(x, axis, [(i, (i + by) % n) for i in range(n)])


def swap(x, dx, dz):
    nx, nz = lax.axis_size("x"), lax.axis_size("zh")
    pairs = [
        (a * nz + b, ((a + dx) % nx) * nz + (b + dz) % nz) for a in range(nx) for b in range(nz)
    ]
    return lax.ppermute(x, ("x", "zh"), pairs)


def ordered(zh, keep, got, axis):
    first = jnp.where(zh == 0, keep, got)
    second = jnp.where(zh == 0, got, keep)
    return jnp.concatenate([first, second], axis=axis)


def gather_y(block):
    n = lax.axis_size("y")
    me = lax.axis_index("y")
    rows = block.shape[0]
    full = jnp.zeros((n,) + block.shape, block.dtype)

    def put(full, part, owner, row=0):
        return lax.dynamic_update_slice(full, part[None], (owner % n, row, 0))

    full = put(full, block, me)
    right = left = block
    for step in range(1, n // 2):
        right = shift(right, "y", 1)
        left = shift(left, "y", -1)
        full = put(full, right, me - step + n)
        full = put(full, left, me + step)
    half = rows // 2
    far = me + n // 2
    full = put(full, shift(right[:half], "y", 1), far)
    full = put(full, shift(left[half:], "y", -1), far, half)
    return full


def forward_kernel(ft_ref, w_ref, g_ref, gain_ref, img_ref, a_ref, b_ref, stat_ref, acc_ref):
    step = pl.program_id(0)

    @pl.when(step == 0)
    def _():
        acc_ref[...] = jnp.zeros_like(acc_ref)

    for c in range(2):
        total = acc_ref[c]
        for j in range(ft_ref.shape[0]):
            total += jnp.dot(ft_ref[j], w_ref[c, j], preferred_element_type=F32)
        acc_ref[c] = total

    @pl.when(step == pl.num_programs(0) - 1)
    def _():
        square = jnp.zeros((1, HALF), F32)
        cross = jnp.zeros((1, HALF), F32)
        for c in range(2):
            v = acc_ref[c].T
            v2 = v * v
            t = jnp.tanh(GELU_K * (v + GELU_C * v2 * v))
            image = (0.5 * v * (1.0 + t)).astype(BF)
            slope = 0.5 * (1.0 + t) + 0.5 * v * (1.0 - t * t) * GELU_K * (
                1.0 + 3.0 * GELU_C * v2
            )
            img_ref[c] = image
            m = image.astype(F32)
            cot = g_ref[c].astype(F32) * gain_ref[c]
            square += jnp.sum(m * m, axis=0, keepdims=True)
            cross += jnp.sum(cot * m, axis=0, keepdims=True)
            a_ref[c] = slope * cot
            b_ref[c] = slope * m
        stat_ref[0:1] = square
        stat_ref[1:2] = cross


def forward(ft, w, g, gain, per_step=8):
    steps = ft.shape[0] // per_step
    full = lambda *s: pl.BlockSpec(s, lambda i: (0,) * len(s))
    return pl.pallas_call(
        forward_kernel,
        grid=(steps,),
        in_specs=[
            pl.BlockSpec((per_step, HALF, ROWS_PAD), lambda i: (i, 0, 0)),
            pl.BlockSpec((2, per_step, ROWS_PAD, COLS_PAD), lambda i: (0, i, 0, 0)),
            full(2, COLS_PAD, HALF),
            full(2, COLS_PAD, 1),
        ],
        out_specs=[
            full(2, COLS_PAD, HALF),
            full(2, COLS_PAD, HALF),
            full(2, COLS_PAD, HALF),
            full(2, HALF),
        ],
        out_shape=[
            jax.ShapeDtypeStruct((2, COLS_PAD, HALF), BF),
            jax.ShapeDtypeStruct((2, COLS_PAD, HALF), F32),
            jax.ShapeDtypeStruct((2, COLS_PAD, HALF), F32),
            jax.ShapeDtypeStruct((2, HALF), F32),
        ],
        scratch_shapes=[pltpu.VMEM((2, HALF, COLS_PAD), F32)],
        compiler_params=pltpu.CompilerParams(vmem_limit_bytes=48 << 20),
        name="forward",
    )(ft, w, g, gain)


def backward_kernel(width, w_ref, a_ref, b_ref, img_ref, gain_ref, stat_ref, p_ref, n_ref, gp_ref):
    @pl.when(pl.program_id(0) == 0)
    def _():
        inv = lax.rsqrt(stat_ref[0:1] / width + EPS)
        back = inv * inv * inv * stat_ref[1:2] / width
        for c in range(2):
            gp_ref[c] = (inv * a_ref[c] - back * b_ref[c]).astype(BF)
            n_ref[c] = (img_ref[c].astype(F32) * inv * gain_ref[c]).astype(BF)

    for j in range(p_ref.shape[0]):
        p = jnp.dot(w_ref[0, j], gp_ref[0], preferred_element_type=F32)
        p += jnp.dot(w_ref[1, j], gp_ref[1], preferred_element_type=F32)
        p_ref[j] = p.astype(BF)


def backward(w, a, b, image, gain, stat, width, per_step=8):
    steps = w.shape[1] // per_step
    full = lambda *s: pl.BlockSpec(s, lambda i: (0,) * len(s))
    return pl.pallas_call(
        functools.partial(backward_kernel, width),
        grid=(steps,),
        in_specs=[
            pl.BlockSpec((2, per_step, ROWS_PAD, COLS_PAD), lambda i: (0, i, 0, 0)),
            full(2, COLS_PAD, HALF),
            full(2, COLS_PAD, HALF),
            full(2, COLS_PAD, HALF),
            full(2, COLS_PAD, 1),
            full(2, HALF),
        ],
        out_specs=[
            pl.BlockSpec((per_step, ROWS_PAD, HALF), lambda i: (i, 0, 0)),
            full(2, COLS_PAD, HALF),
        ],
        out_shape=[
            jax.ShapeDtypeStruct((w.shape[1], ROWS_PAD, HALF), BF),
            jax.ShapeDtypeStruct((2, COLS_PAD, HALF), BF),
        ],
        scratch_shapes=[pltpu.VMEM((2, COLS_PAD, HALF), BF)],
        compiler_params=pltpu.CompilerParams(vmem_limit_bytes=48 << 20),
        name="backward",
    )(w, a, b, image, gain, stat)


def per_device(sig_feat, conv_feat, weight, gain, text, grad_out, tile_count, tile_block):
    zh = lax.axis_index("zh")
    n_y = lax.axis_size("y")
    n_dp = lax.axis_size("x") * lax.axis_size("zl") * lax.axis_size("core")
    slots, tile_tokens = sig_feat.shape[:2]
    tokens = slots * tile_tokens
    model_width = COLS * n_y * 2

    g0 = gain.astype(BF)
    g1 = (gain - g0.astype(F32)).astype(BF)
    g2 = (gain - g0.astype(F32) - g1.astype(F32)).astype(BF)
    spare = jnp.stack([g0, g1, g2, jnp.zeros_like(g0)])
    w_own = jnp.pad(jnp.concatenate([weight, spare]), ((0, 0), (0, COLS_PAD - COLS)))
    w_all = lax.all_gather(w_own, ("zh", "x", "zl", "core"), axis=0)
    w_all = w_all.reshape(2, n_dp, ROWS_PAD, COLS_PAD)

    def half_of(x, which):
        return lax.dynamic_slice_in_dim(x, which * HALF, HALF, 1)

    sig_t = sig_feat.reshape(tokens, SIG).T
    conv_t = conv_feat.reshape(tokens, CONV).T
    half_way = lax.axis_size("x") // 2
    sig_got = swap(half_of(sig_t, 1 - zh), 0, 1)
    conv_got = swap(half_of(conv_t, 1 - zh), half_way, 1)
    conv_keep = swap(half_of(conv_t, zh), half_way, 0)
    block = jnp.concatenate(
        [
            ordered(zh, half_of(sig_t, zh), sig_got, 0),
            ordered(zh, conv_keep, conv_got, 0),
        ]
    )
    feats = gather_y(block)
    feats = jnp.concatenate(
        [feats[:, : 2 * SIG].reshape(-1, HALF), feats[:, 2 * SIG :].reshape(-1, HALF)]
    )
    feats = feats.reshape(n_dp, ROWS, HALF).transpose(0, 2, 1)
    feats = jnp.pad(feats, ((0, 0), (0, 0), (0, ROWS_PAD - ROWS)))

    live = jnp.arange(slots, dtype=jnp.int32) < tile_count[0]
    block_of = jnp.where(live, tile_block[0, :slots], -1)
    slot_block = jnp.repeat(block_of, tile_tokens)
    place = jnp.arange(tokens, dtype=jnp.int32) % tile_tokens
    seq_block = jnp.arange(tokens, dtype=jnp.int32) // tile_tokens
    chooser = (
        (slot_block[:, None] == seq_block[None, :]) & (place[:, None] == place[None, :])
    ).astype(BF)
    is_image = jnp.any(block_of[:, None] == jnp.arange(slots, dtype=jnp.int32)[None, :], axis=0)
    is_image = jnp.repeat(is_image, tile_tokens)

    text_t = text.T
    grad_t = grad_out.T
    grad_slots = lax.dot_general(
        grad_t, chooser, (((1,), (1,)), ((), ())), preferred_element_type=F32
    ).astype(BF)
    grad_got = swap(half_of(grad_slots, 1 - zh), 0, 1)
    g = ordered(zh, half_of(grad_slots, zh)[None], grad_got[None], 0)
    g = jnp.pad(g, ((0, 0), (0, COLS_PAD - COLS), (0, 0)))

    spare = w_all[:, 0, ROWS : ROWS + 3].astype(F32)
    gain_pair = (spare[:, 0] + spare[:, 1] + spare[:, 2])[:, :, None]

    image, a, b, stat = forward(feats, w_all, g, gain_pair)

    text_f = text_t.astype(F32)
    text_square = jnp.sum(text_f * text_f, axis=0)
    sums = lax.psum(jnp.concatenate([stat.reshape(-1), text_square]), "y")
    stat = sums[: 2 * HALF].reshape(2, HALF)
    text_square = sums[2 * HALF :]

    p, n_image = backward(w_all, a, b, image, gain_pair, stat, float(model_width))
    p = p[:, :ROWS].reshape(n_dp * ROWS, HALF)
    sig_total = SIG * 2 * n_y
    p = jnp.concatenate(
        [
            p[:sig_total].reshape(n_y, 2 * SIG, HALF),
            p[sig_total:].reshape(n_y, 2 * CONV, HALF),
        ],
        axis=1,
    ).reshape(n_dp * ROWS, HALF)
    grads = lax.psum_scatter(p, "y", scatter_dimension=0, tiled=True)

    n_image = n_image[:, :COLS]
    n_keep = lax.dynamic_index_in_dim(n_image, zh, 0, keepdims=False)
    n_got = swap(lax.dynamic_index_in_dim(n_image, 1 - zh, 0, keepdims=False), 0, 1)
    n_slots = ordered(zh, n_keep, n_got, 1)
    n_placed = jnp.dot(n_slots, chooser, preferred_element_type=F32).astype(BF)
    text_square = text_square + shift(text_square, "zh", 1)
    inv_text = lax.rsqrt(text_square / model_width + EPS)
    n_text = (text_f * inv_text[None, :] * gain[:, None]).astype(BF)
    normed = jnp.where(is_image[None, :], n_placed, n_text).T

    sig_g = grads[: 2 * SIG].reshape(2, SIG, HALF)
    conv_g = grads[2 * SIG :].reshape(2, CONV, HALF)

    def pick(x, which):
        return lax.dynamic_index_in_dim(x, which, 0, keepdims=False)

    sig_got = swap(pick(sig_g, 1 - zh), 0, 1)
    conv_got = swap(pick(conv_g, 1 - zh), half_way, 1)
    conv_keep = swap(pick(conv_g, zh), half_way, 0)
    grad_sig = ordered(zh, pick(sig_g, zh), sig_got, 1).T.reshape(slots, tile_tokens, SIG)
    grad_conv = ordered(zh, conv_keep, conv_got, 1).T.reshape(slots, tile_tokens, CONV)
    return normed, grad_sig, grad_conv


def solution(mesh):
    fine = Mesh(mesh.devices.reshape(4, 4, 2, 8, 2), AXES)
    dp, mp = ("x", "zl", "core"), ("y", "zh")
    return jax.shard_map(
        per_device,
        mesh=fine,
        in_specs=(
            P(dp, None, mp),
            P(dp, None, mp),
            P(dp, mp),
            P(mp),
            P(dp, mp),
            P(dp, mp),
            P(dp),
            P(dp, None),
        ),
        out_specs=(P(dp, mp), P(dp, None, mp), P(dp, None, mp)),
        check_vma=False,
    )
```

```python
import functools

import jax
import jax.numpy as jnp
from jax import lax
from jax.experimental import pallas as pl
from jax.experimental.pallas import tpu as pltpu
from jax.sharding import Mesh
from jax.sharding import PartitionSpec as P

BF = jnp.bfloat16
F32 = jnp.float32
EPS = 1e-05
GELU_K = 0.7978845608
GELU_C = 0.044715

AXES = ("xh", "xl", "zl", "core", "y", "zh")
SIZES = (2, 2, 4, 2, 8, 2)
N_X, N_ZL, N_Y = 4, 4, 8
ROWS = 132
ROWS_PAD = 136
DEEP = N_X * ROWS_PAD
TOTAL = 4224
COLS = 448
COLS_PAD = 512
HALF = 256
SIG = 72
CONV = 192
PAIR_SIG, PAIR_CONV = 2 * SIG, 2 * CONV
PAIR = PAIR_SIG + PAIR_CONV
VMEM_LIMIT = 34 << 20

VMEM = pl.BlockSpec(memory_space=pltpu.VMEM)
SMEM = pl.BlockSpec(memory_space=pltpu.SMEM)


def shift(x, axis, by):
    n = lax.axis_size(axis)
    return lax.ppermute(x, axis, [(i, (i + by) % n) for i in range(n)])


def ordered(zh, keep, got, axis):
    first = jnp.where(zh == 0, keep, got)
    second = jnp.where(zh == 0, got, keep)
    return jnp.concatenate([first, second], axis=axis)


def gather_y(block):
    n = lax.axis_size("y")
    me = lax.axis_index("y")
    rows = block.shape[0]
    full = jnp.zeros((n,) + block.shape, block.dtype)

    def put(full, part, owner, row=0):
        return lax.dynamic_update_slice(full, part[None], (owner % n, row, 0))

    full = put(full, block, me)
    right = left = block
    for step in range(1, n // 2):
        right = shift(right, "y", 1)
        left = shift(left, "y", -1)
        full = put(full, right, me - step + n)
        full = put(full, left, me + step)
    half = rows // 2
    far = me + n // 2
    full = put(full, shift(right[:half], "y", 1), far)
    full = put(full, shift(left[half:], "y", -1), far, half)
    return full


def exchange(sig, conv):
    xh = lax.axis_index("xh")
    sig = jnp.pad(sig, ((0, 0), (0, CONV - SIG), (0, 0)))
    first = jnp.where(xh == 0, sig, conv)
    second = jnp.where(xh == 0, conv, sig)
    got = lax.all_to_all(
        jnp.concatenate([first, second]), ("xh", "zh"), split_axis=0, concat_axis=0, tiled=True
    )
    got = got.reshape((2, 2) + conv.shape[1:])
    return (
        jnp.where(xh == 0, got[0, :, :SIG], got[1, :, :SIG]),
        jnp.where(xh == 0, got[1], got[0]),
    )


def forward_kernel(
    at_ref, feat_ref, g_ref, gain_ref, mine_ref, other_ref,
    img_ref, a_ref, b_ref, stat_ref, nat_ref, part_ref, fp_ref, acc_ref,
):
    for y in range(N_Y):
        nat_ref[PAIR_SIG * y : PAIR_SIG * (y + 1)] = feat_ref[y, :PAIR_SIG].astype(F32)
        base = PAIR_SIG * N_Y + PAIR_CONV * y
        nat_ref[base : base + PAIR_CONV] = feat_ref[y, PAIR_SIG:].astype(F32)
    for x in range(N_X):
        part_ref[x * ROWS_PAD + ROWS : (x + 1) * ROWS_PAD] = jnp.zeros(
            (ROWS_PAD - ROWS, HALF), F32
        )
    for c in range(2):
        for z in range(N_ZL):
            for x in range(N_X):
                row = ((x * N_ZL + z) * 2 + c) * ROWS
                part_ref[x * ROWS_PAD : x * ROWS_PAD + ROWS] = nat_ref[row : row + ROWS]
            fp_ref[c, z] = part_ref[...].astype(BF)
    core = at_ref[0]
    for c in range(2):
        for k, (w_ref, which) in enumerate(((mine_ref, core), (other_ref, 1 - core))):
            for z in range(N_ZL):
                term = lax.dot_general(
                    fp_ref[which, z],
                    w_ref[c * N_ZL + z],
                    (((0,), (0,)), ((), ())),
                    preferred_element_type=F32,
                )
                if k == 0 and z == 0:
                    acc_ref[...] = term
                else:
                    acc_ref[...] += term
        v = acc_ref[...].T
        v2 = v * v
        t = jnp.tanh(GELU_K * (v + GELU_C * v2 * v))
        image = (0.5 * v * (1.0 + t)).astype(BF)
        slope = 0.5 * (1.0 + t) + 0.5 * v * (1.0 - t * t) * GELU_K * (1.0 + 3.0 * GELU_C * v2)
        img_ref[c] = image
        m = image.astype(F32)
        cot = g_ref[c].astype(F32) * gain_ref[c]
        square = jnp.sum(m * m, axis=0, keepdims=True)
        cross = jnp.sum(cot * m, axis=0, keepdims=True)
        a_ref[c] = slope * cot
        b_ref[c] = slope * m
        if c == 0:
            stat_ref[0:1] = square
            stat_ref[1:2] = cross
        else:
            stat_ref[0:1] += square
            stat_ref[1:2] += cross


def forward(at, feats, g, gain, mine, other):
    return pl.pallas_call(
        forward_kernel,
        in_specs=[SMEM] + [VMEM] * 5,
        out_specs=[VMEM] * 4,
        out_shape=[
            jax.ShapeDtypeStruct((2, COLS_PAD, HALF), BF),
            jax.ShapeDtypeStruct((2, COLS_PAD, HALF), F32),
            jax.ShapeDtypeStruct((2, COLS_PAD, HALF), F32),
            jax.ShapeDtypeStruct((2, HALF), F32),
        ],
        scratch_shapes=[
            pltpu.VMEM((TOTAL, HALF), F32),
            pltpu.VMEM((DEEP, HALF), F32),
            pltpu.VMEM((2, N_ZL, DEEP, HALF), BF),
            pltpu.VMEM((HALF, COLS_PAD), F32),
        ],
        compiler_params=pltpu.CompilerParams(vmem_limit_bytes=VMEM_LIMIT),
        name="forward",
    )(at, feats, g, gain, mine, other)


def backward_kernel(
    width, at_ref, a_ref, b_ref, img_ref, gain_ref, stat_ref, mine_ref, other_ref,
    p_ref, n_ref, gp_ref, pp_ref, nat_ref,
):
    stat = jnp.sum(stat_ref[...], axis=0)
    inv = lax.rsqrt(stat[0:1] / width + EPS)
    back = inv * inv * inv * stat[1:2] / width
    for c in range(2):
        gp_ref[c] = (inv * a_ref[c] - back * b_ref[c]).astype(BF)
        n_ref[c] = (img_ref[c].astype(F32) * inv * gain_ref[c]).astype(BF)
    core = at_ref[0]
    for w_ref, which in ((mine_ref, core), (other_ref, 1 - core)):
        for z in range(N_ZL):
            p = jnp.dot(w_ref[z], gp_ref[0], preferred_element_type=F32)
            p += jnp.dot(w_ref[N_ZL + z], gp_ref[1], preferred_element_type=F32)
            pp_ref[which, z] = p
    for c in range(2):
        for z in range(N_ZL):
            for x in range(N_X):
                row = ((x * N_ZL + z) * 2 + c) * ROWS
                nat_ref[row : row + ROWS] = pp_ref[c, z, x * ROWS_PAD : x * ROWS_PAD + ROWS]
    for y in range(N_Y):
        p_ref[y, :PAIR_SIG] = nat_ref[PAIR_SIG * y : PAIR_SIG * (y + 1)].astype(BF)
        base = PAIR_SIG * N_Y + PAIR_CONV * y
        p_ref[y, PAIR_SIG:] = nat_ref[base : base + PAIR_CONV].astype(BF)


def backward(at, a, b, image, gain, stat, mine, other, width):
    return pl.pallas_call(
        functools.partial(backward_kernel, width),
        in_specs=[SMEM] + [VMEM] * 7,
        out_specs=[VMEM] * 2,
        out_shape=[
            jax.ShapeDtypeStruct((N_Y, PAIR, HALF), BF),
            jax.ShapeDtypeStruct((2, COLS_PAD, HALF), BF),
        ],
        scratch_shapes=[
            pltpu.VMEM((2, COLS_PAD, HALF), BF),
            pltpu.VMEM((2, N_ZL, DEEP, HALF), F32),
            pltpu.VMEM((TOTAL, HALF), F32),
        ],
        compiler_params=pltpu.CompilerParams(vmem_limit_bytes=VMEM_LIMIT),
        name="backward",
    )(at, a, b, image, gain, stat, mine, other)


def per_device(sig_feat, conv_feat, weight, gain, text, grad_out, tile_count, tile_block):
    zh = lax.axis_index("zh")
    slots, tile_tokens = sig_feat.shape[:2]
    tokens = slots * tile_tokens
    model_width = COLS * N_Y * 2
    at = lax.axis_index("core").astype(jnp.int32).reshape(1)

    g0 = gain.astype(BF)
    g1 = (gain - g0.astype(F32)).astype(BF)
    g2 = (gain - g0.astype(F32) - g1.astype(F32)).astype(BF)
    spare = jnp.stack([g0, g1, g2, jnp.zeros_like(g0)])
    w_own = jnp.pad(jnp.concatenate([weight, spare]), ((0, 0), (0, COLS_PAD - COLS)))
    w_x = lax.all_gather(w_own, ("xh", "xl"), axis=0)
    w_x, sig_feat, conv_feat = lax.optimization_barrier((w_x, sig_feat, conv_feat))
    mine = lax.all_gather(w_x.reshape(DEEP, COLS_PAD), ("zh", "zl"), axis=0)

    def by_half(x):
        return jnp.stack([x[:, :HALF], x[:, HALF:]])

    sig, conv = exchange(
        by_half(sig_feat.reshape(tokens, SIG).T), by_half(conv_feat.reshape(tokens, CONV).T)
    )
    feats = gather_y(
        jnp.concatenate([sig.reshape(PAIR_SIG, HALF), conv.reshape(PAIR_CONV, HALF)])
    )

    live = jnp.arange(slots, dtype=jnp.int32) < tile_count[0]
    block_of = jnp.where(live, tile_block[0, :slots], -1)
    slot_block = jnp.repeat(block_of, tile_tokens)
    place = jnp.arange(tokens, dtype=jnp.int32) % tile_tokens
    seq_block = jnp.arange(tokens, dtype=jnp.int32) // tile_tokens
    chooser = (
        (slot_block[:, None] == seq_block[None, :]) & (place[:, None] == place[None, :])
    ).astype(BF)
    is_image = jnp.any(block_of[:, None] == jnp.arange(slots, dtype=jnp.int32)[None, :], axis=0)
    is_image = jnp.repeat(is_image, tile_tokens)

    def half_of(x, which):
        return lax.dynamic_slice_in_dim(x, which * HALF, HALF, 1)

    grad_slots = lax.dot_general(
        grad_out.T, chooser, (((1,), (1,)), ((), ())), preferred_element_type=F32
    ).astype(BF)
    grad_got = shift(half_of(grad_slots, 1 - zh), "zh", 1)
    g = ordered(zh, half_of(grad_slots, zh)[None], grad_got[None], 0)
    g = jnp.pad(g, ((0, 0), (0, COLS_PAD - COLS), (0, 0)))

    mine, feats, g = lax.optimization_barrier((mine, feats, g))
    other = shift(mine, "core", 1)
    spare = mine[::N_ZL, ROWS : ROWS + 3].astype(F32)
    gain_pair = (spare[:, 0] + spare[:, 1] + spare[:, 2])[:, :, None]

    image, a, b, stat = forward(at, feats, g, gain_pair, mine, other)
    stat = lax.all_to_all(
        jnp.broadcast_to(stat[None], (N_Y,) + stat.shape), "y", 0, 0, tiled=True
    )
    p, n_image = backward(at, a, b, image, gain_pair, stat, mine, other, float(model_width))
    text_f = text.T.astype(F32)
    text_square, p = lax.optimization_barrier((jnp.sum(text_f * text_f, axis=0), p))
    grads = lax.psum_scatter(
        p.reshape(TOTAL, HALF), "y", scatter_dimension=0, tiled=True
    )

    n_image = n_image[:, :COLS]
    n_keep = lax.dynamic_index_in_dim(n_image, zh, 0, keepdims=False)
    n_got = shift(lax.dynamic_index_in_dim(n_image, 1 - zh, 0, keepdims=False), "zh", 1)
    n_slots = ordered(zh, n_keep, n_got, 1)
    n_placed = jnp.dot(n_slots, chooser, preferred_element_type=F32).astype(BF)
    text_square = lax.psum(text_square, "y")
    text_square = text_square + shift(text_square, "zh", 1)
    inv_text = lax.rsqrt(text_square / model_width + EPS)
    n_text = (text_f * inv_text[None, :] * gain[:, None]).astype(BF)
    normed = jnp.where(is_image[None, :], n_placed, n_text).T

    sig_g, conv_g = exchange(
        grads[:PAIR_SIG].reshape(2, SIG, HALF), grads[PAIR_SIG:].reshape(2, CONV, HALF)
    )

    def tokens_first(x, width):
        return jnp.concatenate([x[0], x[1]], axis=1).T.reshape(slots, tile_tokens, width)

    return normed, tokens_first(sig_g, SIG), tokens_first(conv_g, CONV)


def solution(mesh):
    fine = Mesh(mesh.devices.reshape(SIZES), AXES)
    dp, mp = ("xh", "xl", "zl", "core"), ("y", "zh")
    return jax.shard_map(
        per_device,
        mesh=fine,
        in_specs=(
            P(dp, None, mp),
            P(dp, None, mp),
            P(dp, mp),
            P(mp),
            P(dp, mp),
            P(dp, mp),
            P(dp),
            P(dp, None),
        ),
        out_specs=(P(dp, mp), P(dp, None, mp), P(dp, None, mp)),
        check_vma=False,
    )
```

```python
import functools

import jax
import jax.numpy as jnp
from jax import lax
from jax.experimental import pallas as pl
from jax.experimental.pallas import tpu as pltpu
from jax.sharding import Mesh
from jax.sharding import PartitionSpec as P

BF = jnp.bfloat16
F32 = jnp.float32
EPS = 1e-05
GELU_K = 0.7978845608
GELU_C = 0.044715

AXES = ("xh", "xl", "zl", "core", "y", "zh")
SIZES = (2, 2, 4, 2, 8, 2)
N_X, N_ZL, N_Y = 4, 4, 8
ROWS = 132
ROWS_PAD = 136
DEEP = N_X * ROWS_PAD
TOTAL = 4224
COLS = 448
COLS_PAD = 512
HALF = 256
SIG = 72
CONV = 192
PAIR_SIG, PAIR_CONV = 2 * SIG, 2 * CONV
PAIR = PAIR_SIG + PAIR_CONV

VMEM = pl.BlockSpec(memory_space=pltpu.VMEM)
SMEM = pl.BlockSpec(memory_space=pltpu.SMEM)


def shift(x, axis, by):
    n = lax.axis_size(axis)
    return lax.ppermute(x, axis, [(i, (i + by) % n) for i in range(n)])


def ordered(zh, keep, got, axis):
    first = jnp.where(zh == 0, keep, got)
    second = jnp.where(zh == 0, got, keep)
    return jnp.concatenate([first, second], axis=axis)


def gather_y(block):
    n = lax.axis_size("y")
    me = lax.axis_index("y")
    rows = block.shape[0]
    full = jnp.zeros((n,) + block.shape, block.dtype)

    def put(full, part, owner, row=0):
        return lax.dynamic_update_slice(full, part[None], (owner % n, row, 0))

    full = put(full, block, me)
    right = left = block
    for step in range(1, n // 2):
        right = shift(right, "y", 1)
        left = shift(left, "y", -1)
        full = put(full, right, me - step + n)
        full = put(full, left, me + step)
    half = rows // 2
    far = me + n // 2
    full = put(full, shift(right[:half], "y", 1), far)
    full = put(full, shift(left[half:], "y", -1), far, half)
    return full


def exchange(blocks):
    xh = lax.axis_index("xh")
    got = lax.all_to_all(blocks, ("xh", "zh"), split_axis=0, concat_axis=0, tiled=True)
    got = got.reshape((2, 2) + blocks.shape[1:])
    return (
        jnp.where(xh == 0, got[0, :, :SIG], got[1, :, :SIG]),
        jnp.where(xh == 0, got[1], got[0]),
    )


def call(kernel, name, limit, out_shape, scratch, flops, *args):
    moved = sum(x.size * x.dtype.itemsize for x in args)
    moved += sum(x.size * x.dtype.itemsize for x in out_shape)
    return pl.pallas_call(
        kernel,
        in_specs=[SMEM] + [VMEM] * (len(args) - 1),
        out_specs=[VMEM] * len(out_shape),
        out_shape=out_shape,
        scratch_shapes=scratch,
        compiler_params=pltpu.CompilerParams(vmem_limit_bytes=limit << 20),
        cost_estimate=pl.CostEstimate(flops=flops, bytes_accessed=moved, transcendentals=0),
        name=name,
    )(*args)


def shaped(dtype, *shape):
    return jax.ShapeDtypeStruct(shape, dtype)


def rows_of(x, z, c):
    return ((x * N_ZL + z) * 2 + c) * ROWS


def arrange_kernel(at_ref, feat_ref, mine_ref, other_ref, nat_ref, part_ref):
    for y in range(N_Y):
        nat_ref[PAIR_SIG * y : PAIR_SIG * (y + 1)] = feat_ref[y, :PAIR_SIG].astype(F32)
        base = PAIR_SIG * N_Y + PAIR_CONV * y
        nat_ref[base : base + PAIR_CONV] = feat_ref[y, PAIR_SIG:].astype(F32)
    for x in range(N_X):
        part_ref[x * ROWS_PAD + ROWS : (x + 1) * ROWS_PAD] = jnp.zeros(
            (ROWS_PAD - ROWS, HALF), F32
        )
    for c in range(2):
        for z in range(N_ZL):
            for x in range(N_X):
                row = rows_of(x, z, c)
                part_ref[x * ROWS_PAD : x * ROWS_PAD + ROWS] = nat_ref[row : row + ROWS]
            part = part_ref[...].astype(BF)

            @pl.when(at_ref[0] == c)
            def _():
                mine_ref[z] = part

            @pl.when(at_ref[0] != c)
            def _():
                other_ref[z] = part


def arrange(at, feats):
    return call(
        arrange_kernel,
        "arrange",
        16,
        [shaped(BF, N_ZL, DEEP, HALF)] * 2,
        [pltpu.VMEM((TOTAL, HALF), F32), pltpu.VMEM((DEEP, HALF), F32)],
        0,
        at,
        feats,
    )


def products(fp_ref, w_ref, c, total):
    for z in range(N_ZL):
        term = lax.dot_general(
            fp_ref[z], w_ref[c * N_ZL + z], (((0,), (0,)), ((), ())), preferred_element_type=F32
        )
        total = term if total is None else total + term
    return total


def first_kernel(at_ref, fp_ref, w_ref, acc_ref):
    for c in range(2):
        acc_ref[c] = products(fp_ref, w_ref, c, None)


def second_kernel(
    at_ref, fp_ref, w_ref, acc_ref, g_ref, gain_ref, img_ref, a_ref, b_ref, stat_ref
):
    for c in range(2):
        v = products(fp_ref, w_ref, c, acc_ref[c]).T
        v2 = v * v
        t = jnp.tanh(GELU_K * (v + GELU_C * v2 * v))
        image = (0.5 * v * (1.0 + t)).astype(BF)
        slope = 0.5 * (1.0 + t) + 0.5 * v * (1.0 - t * t) * GELU_K * (1.0 + 3.0 * GELU_C * v2)
        img_ref[c] = image
        m = image.astype(F32)
        cot = g_ref[c].astype(F32) * gain_ref[c]
        square = jnp.sum(m * m, axis=0, keepdims=True)
        cross = jnp.sum(cot * m, axis=0, keepdims=True)
        a_ref[c] = slope * cot
        b_ref[c] = slope * m
        if c == 0:
            stat_ref[0:1] = square
            stat_ref[1:2] = cross
        else:
            stat_ref[0:1] += square
            stat_ref[1:2] += cross


def forward(at, fp_mine, fp_other, mine, other, g, gain):
    flops = HALF * TOTAL * COLS * 2
    acc = call(
        first_kernel, "first_half", 14, [shaped(F32, 2, HALF, COLS_PAD)], [], flops,
        at, fp_mine, mine,
    )[0]
    return call(
        second_kernel,
        "second_half",
        18,
        [
            shaped(BF, 2, COLS_PAD, HALF),
            shaped(F32, 2, COLS_PAD, HALF),
            shaped(F32, 2, COLS_PAD, HALF),
            shaped(F32, 2, HALF),
        ],
        [],
        flops,
        at, fp_other, other, acc, g, gain,
    )


def backward_kernel(
    width, at_ref, a_ref, b_ref, img_ref, gain_ref, stat_ref, mine_ref, other_ref,
    sig_ref, conv_ref, n_ref, gp_ref, pp_ref, part_ref,
):
    stat = jnp.sum(stat_ref[:, 0:2], axis=0)
    inv = lax.rsqrt(stat[0:1] / width + EPS)
    back = inv * inv * inv * stat[1:2] / width
    for c in range(2):
        gp_ref[c] = (inv * a_ref[c] - back * b_ref[c]).astype(BF)
        n_ref[c] = (img_ref[c].astype(F32) * inv * gain_ref[c]).astype(BF)
    core = at_ref[0]
    for w_ref, which in ((mine_ref, core), (other_ref, 1 - core)):
        for z in range(N_ZL):
            p = jnp.dot(w_ref[z], gp_ref[0], preferred_element_type=F32)
            p += jnp.dot(w_ref[N_ZL + z], gp_ref[1], preferred_element_type=F32)
            pp_ref[which, z] = p

    def piece(begin, length):
        done = 0
        while done < length:
            owner, skip = divmod(begin + done, ROWS)
            n = min(ROWS - skip, length - done)
            c, z, x = owner % 2, owner // 2 % N_ZL, owner // (2 * N_ZL)
            row = x * ROWS_PAD + skip
            part_ref[done : done + n] = pp_ref[c, z, row : row + n]
            done += n
        return part_ref[:length].astype(BF)

    for y in range(N_Y):
        sig_ref[y] = piece(PAIR_SIG * y, PAIR_SIG)
        conv_ref[y] = piece(PAIR_SIG * N_Y + PAIR_CONV * y, PAIR_CONV)


def backward(at, a, b, image, gain, stat, mine, other, width):
    return call(
        functools.partial(backward_kernel, width),
        "backward",
        24,
        [
            shaped(BF, N_Y, PAIR_SIG, HALF),
            shaped(BF, N_Y, PAIR_CONV, HALF),
            shaped(BF, 2, COLS_PAD, HALF),
        ],
        [
            pltpu.VMEM((2, COLS_PAD, HALF), BF),
            pltpu.VMEM((2, N_ZL, DEEP, HALF), F32),
            pltpu.VMEM((PAIR_CONV, HALF), F32),
        ],
        HALF * TOTAL * COLS * 4,
        at, a, b, image, gain, stat, mine, other,
    )


def pack_kernel(at_ref, sig_ref, conv_ref, out_ref):
    sig = sig_ref[0].astype(F32)
    for y in range(1, N_Y):
        sig += sig_ref[y].astype(F32)
    pad = jnp.zeros((CONV - SIG, HALF), F32)
    for b in range(2):
        out_ref[at_ref[0], b] = jnp.concatenate([sig[b * SIG : (b + 1) * SIG], pad]).astype(BF)
        out_ref[1 - at_ref[0], b] = conv_ref[b * CONV : (b + 1) * CONV]


def pack(xh, sig, conv):
    return call(
        pack_kernel, "pack", 8, [shaped(BF, 2, 2, CONV, HALF)], [], 0,
        xh.astype(jnp.int32).reshape(1), sig, conv,
    )[0].reshape(4, CONV, HALF)


def per_device(sig_feat, conv_feat, weight, gain, text, grad_out, tile_count, tile_block):
    zh = lax.axis_index("zh")
    slots, tile_tokens = sig_feat.shape[:2]
    tokens = slots * tile_tokens
    model_width = COLS * N_Y * 2
    at = lax.axis_index("core").astype(jnp.int32).reshape(1)

    g0 = gain.astype(BF)
    g1 = (gain - g0.astype(F32)).astype(BF)
    g2 = (gain - g0.astype(F32) - g1.astype(F32)).astype(BF)
    spare = jnp.stack([g0, g1, g2, jnp.zeros_like(g0)])
    w_own = jnp.pad(jnp.concatenate([weight, spare]), ((0, 0), (0, COLS_PAD - COLS)))
    w_x = lax.all_gather(w_own, ("xh", "xl"), axis=0)
    w_x, sig_feat, conv_feat = lax.optimization_barrier((w_x, sig_feat, conv_feat))
    mine = lax.all_gather(w_x.reshape(DEEP, COLS_PAD), ("zh", "zl"), axis=0)

    def by_half(x):
        return jnp.stack([x[:, :HALF], x[:, HALF:]])

    xh = lax.axis_index("xh")
    sig = by_half(sig_feat.reshape(tokens, SIG).T)
    conv = by_half(conv_feat.reshape(tokens, CONV).T)
    sig = jnp.pad(sig, ((0, 0), (0, CONV - SIG), (0, 0)))
    sig, conv = exchange(
        jnp.concatenate([jnp.where(xh == 0, sig, conv), jnp.where(xh == 0, conv, sig)])
    )
    feats = gather_y(
        jnp.concatenate([sig.reshape(PAIR_SIG, HALF), conv.reshape(PAIR_CONV, HALF)])
    )

    live = jnp.arange(slots, dtype=jnp.int32) < tile_count[0]
    block_of = jnp.where(live, tile_block[0, :slots], -1)
    slot_block = jnp.repeat(block_of, tile_tokens)
    place = jnp.arange(tokens, dtype=jnp.int32) % tile_tokens
    seq_block = jnp.arange(tokens, dtype=jnp.int32) // tile_tokens
    chooser = (
        (slot_block[:, None] == seq_block[None, :]) & (place[:, None] == place[None, :])
    ).astype(BF)
    is_image = jnp.any(block_of[:, None] == jnp.arange(slots, dtype=jnp.int32)[None, :], axis=0)
    is_image = jnp.repeat(is_image, tile_tokens)

    def half_of(x, which):
        return lax.dynamic_slice_in_dim(x, which * HALF, HALF, 1)

    grad_slots = lax.dot_general(
        grad_out.T, chooser, (((1,), (1,)), ((), ())), preferred_element_type=F32
    ).astype(BF)
    fp_mine, fp_other = arrange(at, feats)
    mine, fp_mine, fp_other, grad_keep, grad_give = lax.optimization_barrier(
        (mine, fp_mine, fp_other, half_of(grad_slots, zh), half_of(grad_slots, 1 - zh))
    )
    other = shift(mine, "core", 1)
    grad_got = shift(grad_give, "zh", 1)
    g = ordered(zh, grad_keep[None], grad_got[None], 0)
    g = jnp.pad(g, ((0, 0), (0, COLS_PAD - COLS), (0, 0)))
    spare = mine[::N_ZL, ROWS : ROWS + 3].astype(F32)
    gain_pair = (spare[:, 0] + spare[:, 1] + spare[:, 2])[:, :, None]

    image, a, b, stat = forward(at, fp_mine, fp_other, mine, other, g, gain_pair)
    text_f = text.T.astype(F32)
    text_square = jnp.sum(text_f * text_f, axis=0).reshape(2, HALF)
    stat = jnp.concatenate([stat, text_square])
    stat = lax.all_to_all(
        jnp.broadcast_to(stat[None], (N_Y,) + stat.shape), "y", 0, 0, tiled=True
    )
    sig_p, conv_p, n_image = backward(at, a, b, image, gain_pair, stat, mine, other, float(model_width))
    stat, sig_p, conv_p = lax.optimization_barrier((stat, sig_p, conv_p))
    text_square = jnp.sum(stat[:, 2:], axis=0).reshape(tokens)
    conv_p = lax.psum_scatter(
        conv_p.reshape(N_Y * PAIR_CONV, HALF), "y", scatter_dimension=0, tiled=True
    )
    sig_p = lax.all_to_all(sig_p, "y", 0, 0, tiled=True)

    n_image = n_image[:, :COLS]
    n_keep = lax.dynamic_index_in_dim(n_image, zh, 0, keepdims=False)
    n_got = shift(lax.dynamic_index_in_dim(n_image, 1 - zh, 0, keepdims=False), "zh", 1)
    n_slots = ordered(zh, n_keep, n_got, 1)
    n_placed = jnp.dot(n_slots, chooser, preferred_element_type=F32).astype(BF)
    text_square = text_square + shift(text_square, "zh", 1)
    inv_text = lax.rsqrt(text_square / model_width + EPS)
    n_text = (text_f * inv_text[None, :] * gain[:, None]).astype(BF)
    normed = jnp.where(is_image[None, :], n_placed, n_text).T

    sig_g, conv_g = exchange(pack(xh, sig_p, conv_p))

    def tokens_first(x, width):
        return jnp.concatenate([x[0], x[1]], axis=1).T.reshape(slots, tile_tokens, width)

    return normed, tokens_first(sig_g, SIG), tokens_first(conv_g, CONV)


def solution(mesh):
    fine = Mesh(mesh.devices.reshape(SIZES), AXES)
    dp, mp = ("xh", "xl", "zl", "core"), ("y", "zh")
    return jax.shard_map(
        per_device,
        mesh=fine,
        in_specs=(
            P(dp, None, mp),
            P(dp, None, mp),
            P(dp, mp),
            P(mp),
            P(dp, mp),
            P(dp, mp),
            P(dp),
            P(dp, None),
        ),
        out_specs=(P(dp, mp), P(dp, None, mp), P(dp, None, mp)),
        check_vma=False,
    )
```

```python
import functools

import jax
import jax.numpy as jnp
from jax import lax
from jax.experimental import pallas as pl
from jax.experimental.pallas import tpu as pltpu
from jax.sharding import Mesh
from jax.sharding import PartitionSpec as P

BF = jnp.bfloat16
F32 = jnp.float32
EPS = 1e-05
GELU_K = 0.7978845608
GELU_C = 0.044715

AXES = ("xh", "xl", "zl", "core", "y", "zh")
SIZES = (2, 2, 4, 2, 8, 2)
N_X, N_ZL, N_Y = 4, 4, 8
ROWS = 132
DEEP = 2 * ROWS
WIDE = 896
RIGHT = 384
TOTAL = 4224
COLS = 448
COLS_PAD = 512
HALF = 256
SIG = 72
CONV = 192
PAIR_SIG, PAIR_CONV = 2 * SIG, 2 * CONV
PAIR = PAIR_SIG + PAIR_CONV

VMEM = pl.BlockSpec(memory_space=pltpu.VMEM)
SMEM = pl.BlockSpec(memory_space=pltpu.SMEM)


def shift(x, axis, by):
    n = lax.axis_size(axis)
    return lax.ppermute(x, axis, [(i, (i + by) % n) for i in range(n)])


def ordered(zh, keep, got, axis):
    first = jnp.where(zh == 0, keep, got)
    second = jnp.where(zh == 0, got, keep)
    return jnp.concatenate([first, second], axis=axis)


def put(full, part, owner):
    return lax.dynamic_update_slice(full, part[None], (owner % N_Y, 0, 0))


def ring_y(block):
    me = lax.axis_index("y")
    full = put(jnp.zeros((N_Y,) + block.shape, block.dtype), block, me)
    right = left = block
    for step in range(1, N_Y // 2):
        right = shift(right, "y", 1)
        left = shift(left, "y", -1)
        full = put(full, right, me - step + N_Y)
        full = put(full, left, me + step)
    return full, right


def exchange(blocks):
    xh = lax.axis_index("xh")
    got = lax.all_to_all(blocks, ("xh", "zh"), split_axis=0, concat_axis=0, tiled=True)
    got = got.reshape((2, 2) + blocks.shape[1:])
    return (
        jnp.where(xh == 0, got[0, :, :SIG], got[1, :, :SIG]),
        jnp.where(xh == 0, got[1], got[0]),
    )


def call(kernel, name, limit, out_shape, scratch, flops, *args):
    moved = sum(x.size * x.dtype.itemsize for x in args)
    moved += sum(x.size * x.dtype.itemsize for x in out_shape)
    return pl.pallas_call(
        kernel,
        in_specs=[SMEM] + [VMEM] * (len(args) - 1),
        out_specs=[VMEM] * len(out_shape),
        out_shape=out_shape,
        scratch_shapes=scratch,
        compiler_params=pltpu.CompilerParams(vmem_limit_bytes=limit << 20),
        cost_estimate=pl.CostEstimate(flops=flops, bytes_accessed=moved, transcendentals=0),
        name=name,
    )(*args)


def shaped(dtype, *shape):
    return jax.ShapeDtypeStruct(shape, dtype)


def rows_of(x, z, c):
    return ((x * N_ZL + z) * 2 + c) * ROWS


def arrange_kernel(at_ref, feat_ref, far_ref, mine_ref, other_ref, nat_ref, part_ref):
    for y in range(N_Y):
        nat_ref[PAIR_SIG * y : PAIR_SIG * (y + 1)] = feat_ref[y, :PAIR_SIG].astype(F32)
        base = PAIR_SIG * N_Y + PAIR_CONV * y
        nat_ref[base : base + PAIR_CONV] = feat_ref[y, PAIR_SIG:].astype(F32)
    far = lax.rem(at_ref[1] + N_Y // 2, N_Y)
    row = pl.multiple_of(PAIR_SIG * far, 16)
    nat_ref[pl.ds(row, PAIR_SIG)] = far_ref[:PAIR_SIG].astype(F32)
    row = pl.multiple_of(PAIR_SIG * N_Y + PAIR_CONV * far, 16)
    nat_ref[pl.ds(row, PAIR_CONV)] = far_ref[PAIR_SIG:].astype(F32)
    for c in range(2):
        for z in range(N_ZL):
            for x in range(N_X):
                row = rows_of(x, z, c)
                part_ref[x * ROWS : (x + 1) * ROWS] = nat_ref[row : row + ROWS]
            part = part_ref[...].astype(BF).reshape(2, DEEP, HALF)

            @pl.when(at_ref[0] == c)
            def _():
                mine_ref[z] = part

            @pl.when(at_ref[0] != c)
            def _():
                other_ref[z] = part


def arrange(at, feats, far):
    return call(
        arrange_kernel,
        "arrange",
        16,
        [shaped(BF, N_ZL, 2, DEEP, HALF)] * 2,
        [pltpu.VMEM((TOTAL, HALF), F32), pltpu.VMEM((2 * DEEP, HALF), F32)],
        0,
        at,
        feats,
        far,
    )


def weight_kernel(at_ref, w_ref, out_ref):
    w = w_ref[...].astype(F32)
    left = jnp.concatenate([w[0], w[1]], axis=0)
    right = jnp.concatenate([w[2], w[3]], axis=0)
    out_ref[...] = jnp.concatenate([left, right], axis=1).astype(BF)


def side_by_side(at, w):
    return call(weight_kernel, "side_by_side", 8, [shaped(BF, DEEP, WIDE)], [], 0, at, w)[0]


def products(fp_ref, w_ref, c):
    left = right = None
    for z in range(N_ZL):
        w = w_ref[c * N_ZL + z]
        dims = (((0,), (0,)), ((), ()))
        one = lax.dot_general(fp_ref[z, 0], w[:, :COLS_PAD], dims, preferred_element_type=F32)
        two = lax.dot_general(fp_ref[z, 1], w[:, RIGHT:], dims, preferred_element_type=F32)
        left = one if left is None else left + one
        right = two if right is None else right + two
    return left + pltpu.roll(right, COLS_PAD - (COLS - RIGHT), axis=1)


def first_kernel(at_ref, fp_ref, w_ref, acc_ref):
    for c in range(2):
        acc_ref[c] = products(fp_ref, w_ref, c)


def second_kernel(at_ref, fp_ref, w_ref, acc_ref, img_ref, slope_ref, square_ref):
    square = jnp.zeros((1, HALF), F32)
    for c in range(2):
        v = (acc_ref[c] + products(fp_ref, w_ref, c)).T
        v = jnp.where(lax.broadcasted_iota(jnp.int32, v.shape, 0) < COLS, v, 0.0)
        v2 = v * v
        t = jnp.tanh(GELU_K * (v + GELU_C * v2 * v))
        image = (0.5 * v * (1.0 + t)).astype(BF)
        img_ref[c] = image
        slope_ref[c] = 0.5 * (1.0 + t) + 0.5 * v * (1.0 - t * t) * GELU_K * (
            1.0 + 3.0 * GELU_C * v2
        )
        m = image.astype(F32)
        square += jnp.sum(m * m, axis=0, keepdims=True)
    square_ref[...] = square


def forward(at, fp_mine, fp_other, mine, other):
    flops = HALF * TOTAL * COLS * 2
    acc = call(
        first_kernel, "first_half", 14, [shaped(F32, 2, HALF, COLS_PAD)], [], flops,
        at, fp_mine, mine,
    )[0]
    return call(
        second_kernel,
        "second_half",
        18,
        [
            shaped(BF, 2, COLS_PAD, HALF),
            shaped(F32, 2, COLS_PAD, HALF),
            shaped(F32, 1, HALF),
        ],
        [],
        flops,
        at, fp_other, other, acc,
    )


def sums_kernel(
    at_ref, img_ref, keep_ref, got_ref, gain_ref, square_ref, text_ref,
    stat_ref, cot_ref, gains_ref,
):
    zh = at_ref[0]
    terms = got_ref[COLS : COLS + 16].astype(F32)
    row = terms[0:2] + terms[2:4] + terms[4:6]
    other = jnp.concatenate(
        [jnp.broadcast_to(row[i : i + 1], (8, HALF)).T[:, :1] for i in range(2)]
    )
    gains_ref[zh] = gain_ref[...]
    gains_ref[1 - zh] = other
    rest = jnp.zeros((COLS_PAD - COLS, HALF), F32)
    cot_ref[zh, :COLS] = keep_ref[...].astype(F32) * gain_ref[:COLS]
    cot_ref[zh, COLS:] = rest
    cot_ref[1 - zh, :COLS] = got_ref[:COLS].astype(F32) * other[:COLS]
    cot_ref[1 - zh, COLS:] = rest
    cross = jnp.zeros((1, HALF), F32)
    for c in range(2):
        cross += jnp.sum(cot_ref[c] * img_ref[c].astype(F32), axis=0, keepdims=True)
    for y in range(N_Y):
        stat_ref[y, 0:1] = square_ref[...]
        stat_ref[y, 1:2] = cross
        stat_ref[y, 2:4] = text_ref[...]


def sums(zh, image, keep, got, gain, square, text):
    return call(
        sums_kernel,
        "sums",
        14,
        [
            shaped(F32, N_Y, 4, HALF),
            shaped(F32, 2, COLS_PAD, HALF),
            shaped(F32, 2, COLS_PAD, 1),
        ],
        [],
        0,
        zh, image, keep, got, gain, square, text,
    )


def backward_kernel(
    width, at_ref, slope_ref, img_ref, cot_ref, gain_ref, stat_ref, mine_ref, other_ref,
    sig_ref, conv_ref, n_ref, gp_ref, pp_ref, part_ref,
):
    stat = jnp.sum(stat_ref[:, 0:2], axis=0)
    inv = lax.rsqrt(stat[0:1] / width + EPS)
    back = inv * inv * inv * stat[1:2] / width
    for c in range(2):
        m = img_ref[c].astype(F32)
        gp = (slope_ref[c] * (inv * cot_ref[c] - back * m)).astype(BF)
        gp_ref[c, 0] = gp
        gp_ref[c, 1] = jnp.concatenate([jnp.zeros((COLS - RIGHT, HALF), BF), gp[:COLS]])
        n_ref[c] = (m * inv * gain_ref[c]).astype(BF)
    core = at_ref[0]
    for w_ref, which in ((mine_ref, core), (other_ref, 1 - core)):
        for z in range(N_ZL):
            for h, cols in ((0, slice(0, COLS_PAD)), (1, slice(RIGHT, WIDE))):
                p = jnp.dot(w_ref[z, :, cols], gp_ref[0, h], preferred_element_type=F32)
                p += jnp.dot(w_ref[N_ZL + z, :, cols], gp_ref[1, h], preferred_element_type=F32)
                pp_ref[which, z, h] = p

    def piece(begin, length):
        done = 0
        while done < length:
            owner, skip = divmod(begin + done, ROWS)
            n = min(ROWS - skip, length - done)
            c, z, x = owner % 2, owner // 2 % N_ZL, owner // (2 * N_ZL)
            row = x % 2 * ROWS + skip
            part_ref[done : done + n] = pp_ref[c, z, x // 2, row : row + n]
            done += n
        return part_ref[:length].astype(BF)

    for y in range(N_Y):
        sig_ref[y] = piece(PAIR_SIG * y, PAIR_SIG)
        conv_ref[y] = piece(PAIR_SIG * N_Y + PAIR_CONV * y, PAIR_CONV)


def backward(at, slope, image, cot, gain, stat, mine, other, width):
    return call(
        functools.partial(backward_kernel, width),
        "backward",
        24,
        [
            shaped(BF, N_Y, PAIR_SIG, HALF),
            shaped(BF, N_Y, PAIR_CONV, HALF),
            shaped(BF, 2, COLS_PAD, HALF),
        ],
        [
            pltpu.VMEM((2, 2, COLS_PAD, HALF), BF),
            pltpu.VMEM((2, N_ZL, 2, DEEP, HALF), F32),
            pltpu.VMEM((PAIR_CONV, HALF), F32),
        ],
        HALF * TOTAL * COLS * 4,
        at, slope, image, cot, gain, stat, mine, other,
    )


def pack_kernel(at_ref, sig_ref, conv_ref, out_ref):
    sig = sig_ref[0].astype(F32)
    for y in range(1, N_Y):
        sig += sig_ref[y].astype(F32)
    pad = jnp.zeros((CONV - SIG, HALF), F32)
    for b in range(2):
        out_ref[at_ref[0], b] = jnp.concatenate([sig[b * SIG : (b + 1) * SIG], pad]).astype(BF)
        out_ref[1 - at_ref[0], b] = conv_ref[b * CONV : (b + 1) * CONV]


def pack(xh, sig, conv):
    return call(
        pack_kernel, "pack", 8, [shaped(BF, 2, 2, CONV, HALF)], [], 0,
        xh.astype(jnp.int32).reshape(1), sig, conv,
    )[0].reshape(4, CONV, HALF)


def per_device(sig_feat, conv_feat, weight, gain, text, grad_out, tile_count, tile_block):
    zh = lax.axis_index("zh")
    slots, tile_tokens = sig_feat.shape[:2]
    tokens = slots * tile_tokens
    model_width = COLS * N_Y * 2
    at = jnp.stack([lax.axis_index("core"), lax.axis_index("y")]).astype(jnp.int32)

    w_x = lax.all_gather(weight, ("xh", "xl"), axis=0)
    w_x, sig_feat, conv_feat = lax.optimization_barrier((w_x, sig_feat, conv_feat))
    mine = lax.all_gather(side_by_side(at, w_x), ("zh", "zl"), axis=0)

    def by_half(x):
        return jnp.stack([x[:, :HALF], x[:, HALF:]])

    xh = lax.axis_index("xh")
    sig = by_half(sig_feat.reshape(tokens, SIG).T)
    conv = by_half(conv_feat.reshape(tokens, CONV).T)
    sig = jnp.pad(sig, ((0, 0), (0, CONV - SIG), (0, 0)))
    sig, conv = exchange(
        jnp.concatenate([jnp.where(xh == 0, sig, conv), jnp.where(xh == 0, conv, sig)])
    )
    feats, right = ring_y(
        jnp.concatenate([sig.reshape(PAIR_SIG, HALF), conv.reshape(PAIR_CONV, HALF)])
    )

    live = jnp.arange(slots, dtype=jnp.int32) < tile_count[0]
    block_of = jnp.where(live, tile_block[0, :slots], -1)
    slot_block = jnp.repeat(block_of, tile_tokens)
    place = jnp.arange(tokens, dtype=jnp.int32) % tile_tokens
    seq_block = jnp.arange(tokens, dtype=jnp.int32) // tile_tokens
    chooser = (
        (slot_block[:, None] == seq_block[None, :]) & (place[:, None] == place[None, :])
    ).astype(BF)
    is_image = jnp.any(block_of[:, None] == jnp.arange(slots, dtype=jnp.int32)[None, :], axis=0)
    is_image = jnp.repeat(is_image, tile_tokens)

    def half_of(x, which):
        return lax.dynamic_slice_in_dim(x, which * HALF, HALF, 1)

    grad_slots = lax.dot_general(
        grad_out.T, chooser, (((1,), (1,)), ((), ())), preferred_element_type=F32
    ).astype(BF)
    g0 = gain.astype(BF)
    g1 = (gain - g0.astype(F32)).astype(BF)
    g2 = (gain - g0.astype(F32) - g1.astype(F32)).astype(BF)
    terms = jnp.pad(jnp.stack([g0, g1, g2]), ((0, 0), (0, COLS_PAD - COLS))).reshape(6, HALF)
    give = jnp.concatenate([half_of(grad_slots, 1 - zh), jnp.pad(terms, ((0, 10), (0, 0)))])
    keep = half_of(grad_slots, zh)

    mine, feats, right, give, keep = lax.optimization_barrier(
        (mine, feats, right, give, keep)
    )
    other = shift(mine, "core", 1)
    fp_mine, fp_other = arrange(at, feats, shift(right, "y", 1))
    got = shift(give, "zh", 1)

    image, slope, square = forward(at, fp_mine, fp_other, mine, other)
    image, slope, square, got = lax.optimization_barrier((image, slope, square, got))
    text_f = text.T.astype(F32)
    text_square = jnp.sum(text_f * text_f, axis=0).reshape(2, HALF)
    gain_own = jnp.pad(gain, (0, COLS_PAD - COLS))[:, None]
    stat, cot, gain_pair = sums(
        zh.astype(jnp.int32).reshape(1), image, keep, got, gain_own, square, text_square
    )
    stat = lax.all_to_all(stat, "y", 0, 0, tiled=True)
    sig_p, conv_p, n_image = backward(
        at, slope, image, cot, gain_pair, stat, mine, other, float(model_width)
    )
    stat, sig_p, conv_p = lax.optimization_barrier((stat, sig_p, conv_p))
    text_square = jnp.sum(stat[:, 2:], axis=0).reshape(tokens)
    conv_p = lax.psum_scatter(
        conv_p.reshape(N_Y * PAIR_CONV, HALF), "y", scatter_dimension=0, tiled=True
    )
    sig_p = lax.all_to_all(sig_p, "y", 0, 0, tiled=True)

    n_image = n_image[:, :COLS]
    n_keep = lax.dynamic_index_in_dim(n_image, zh, 0, keepdims=False)
    n_got = shift(lax.dynamic_index_in_dim(n_image, 1 - zh, 0, keepdims=False), "zh", 1)
    n_slots = ordered(zh, n_keep, n_got, 1)
    n_placed = jnp.dot(n_slots, chooser, preferred_element_type=F32).astype(BF)
    text_square = text_square + shift(text_square, "zh", 1)
    inv_text = lax.rsqrt(text_square / model_width + EPS)
    n_text = (text_f * inv_text[None, :] * gain[:, None]).astype(BF)
    normed = jnp.where(is_image[None, :], n_placed, n_text).T

    sig_g, conv_g = exchange(pack(xh, sig_p, conv_p))

    def tokens_first(x, width):
        return jnp.concatenate([x[0], x[1]], axis=1).T.reshape(slots, tile_tokens, width)

    return normed, tokens_first(sig_g, SIG), tokens_first(conv_g, CONV)


def solution(mesh):
    fine = Mesh(mesh.devices.reshape(SIZES), AXES)
    dp, mp = ("xh", "xl", "zl", "core"), ("y", "zh")
    return jax.shard_map(
        per_device,
        mesh=fine,
        in_specs=(
            P(dp, None, mp),
            P(dp, None, mp),
            P(dp, mp),
            P(mp),
            P(dp, mp),
            P(dp, mp),
            P(dp),
            P(dp, None),
        ),
        out_specs=(P(dp, mp), P(dp, None, mp), P(dp, None, mp)),
        check_vma=False,
    )
```

```python
import functools

import jax
import jax.numpy as jnp
from jax import lax
from jax.experimental import pallas as pl
from jax.experimental.pallas import tpu as pltpu
from jax.sharding import Mesh
from jax.sharding import PartitionSpec as P

BF = jnp.bfloat16
F32 = jnp.float32
EPS = 1e-05
GELU_K = 0.7978845608
GELU_C = 0.044715

AXES = ("xh", "xl", "zl", "core", "y", "zh")
SIZES = (2, 2, 4, 2, 8, 2)
N_X, N_ZL, N_Y = 4, 4, 8
ROWS = 132
DEEP = 2 * ROWS
WIDE = 896
RIGHT = 384
TOTAL = 4224
COLS = 448
COLS_PAD = 512
HALF = 256
SIG = 72
CONV = 192
PAIR_SIG, PAIR_CONV = 2 * SIG, 2 * CONV
PAIR = PAIR_SIG + PAIR_CONV

VMEM = pl.BlockSpec(memory_space=pltpu.VMEM)
SMEM = pl.BlockSpec(memory_space=pltpu.SMEM)


def shift(x, axis, by):
    n = lax.axis_size(axis)
    return lax.ppermute(x, axis, [(i, (i + by) % n) for i in range(n)])


def ordered(zh, keep, got, axis):
    first = jnp.where(zh == 0, keep, got)
    second = jnp.where(zh == 0, got, keep)
    return jnp.concatenate([first, second], axis=axis)


def put(full, part, owner):
    return lax.dynamic_update_slice(full, part[None], (owner % N_Y, 0, 0))


def ring_y(block):
    me = lax.axis_index("y")
    full = put(jnp.zeros((N_Y,) + block.shape, block.dtype), block, me)
    right = left = block
    for step in range(1, N_Y // 2):
        right = shift(right, "y", 1)
        left = shift(left, "y", -1)
        full = put(full, right, me - step + N_Y)
        full = put(full, left, me + step)
    return full, right


def swap(x, dx, dz):
    pairs = [(a * 2 + b, (a + dx) % 2 * 2 + (b + dz) % 2) for a in range(2) for b in range(2)]
    return lax.ppermute(x, ("xh", "zh"), pairs)


def exchange(blocks):
    xh = lax.axis_index("xh")
    got = lax.all_to_all(blocks, ("xh", "zh"), split_axis=0, concat_axis=0, tiled=True)
    got = got.reshape((2, 2) + blocks.shape[1:])
    return (
        jnp.where(xh == 0, got[0, :, :SIG], got[1, :, :SIG]),
        jnp.where(xh == 0, got[1], got[0]),
    )


def call(kernel, name, limit, out_shape, scratch, flops, *args):
    moved = sum(x.size * x.dtype.itemsize for x in args)
    moved += sum(x.size * x.dtype.itemsize for x in out_shape)
    return pl.pallas_call(
        kernel,
        in_specs=[SMEM] + [VMEM] * (len(args) - 1),
        out_specs=[VMEM] * len(out_shape),
        out_shape=out_shape,
        scratch_shapes=scratch,
        compiler_params=pltpu.CompilerParams(vmem_limit_bytes=limit << 20),
        cost_estimate=pl.CostEstimate(flops=flops, bytes_accessed=moved, transcendentals=0),
        name=name,
    )(*args)


def shaped(dtype, *shape):
    return jax.ShapeDtypeStruct(shape, dtype)


def rows_of(x, z, c):
    return ((x * N_ZL + z) * 2 + c) * ROWS


def arrange_kernel(at_ref, feat_ref, far_ref, mine_ref, other_ref, nat_ref, part_ref):
    for y in range(N_Y):
        nat_ref[PAIR_SIG * y : PAIR_SIG * (y + 1)] = feat_ref[y, :PAIR_SIG].astype(F32)
        base = PAIR_SIG * N_Y + PAIR_CONV * y
        nat_ref[base : base + PAIR_CONV] = feat_ref[y, PAIR_SIG:].astype(F32)
    far = lax.rem(at_ref[1] + N_Y // 2, N_Y)
    row = pl.multiple_of(PAIR_SIG * far, 16)
    nat_ref[pl.ds(row, PAIR_SIG)] = far_ref[:PAIR_SIG].astype(F32)
    row = pl.multiple_of(PAIR_SIG * N_Y + PAIR_CONV * far, 16)
    nat_ref[pl.ds(row, PAIR_CONV)] = far_ref[PAIR_SIG:].astype(F32)
    for c in range(2):
        for z in range(N_ZL):
            for x in range(N_X):
                row = rows_of(x, z, c)
                part_ref[x * ROWS : (x + 1) * ROWS] = nat_ref[row : row + ROWS]
            part = part_ref[...].astype(BF).reshape(2, DEEP, HALF)

            @pl.when(at_ref[0] == c)
            def _():
                mine_ref[z] = part

            @pl.when(at_ref[0] != c)
            def _():
                other_ref[z] = part


def arrange(at, feats, far):
    return call(
        arrange_kernel,
        "arrange",
        12,
        [shaped(BF, N_ZL, 2, DEEP, HALF)] * 2,
        [pltpu.VMEM((TOTAL, HALF), F32), pltpu.VMEM((2 * DEEP, HALF), F32)],
        HALF * TOTAL * COLS * 8,
        at,
        feats,
        far,
    )


def weight_kernel(at_ref, w_ref, out_ref):
    w = w_ref[...].astype(F32)
    left = jnp.concatenate([w[0], w[1]], axis=0)
    right = jnp.concatenate([w[2], w[3]], axis=0)
    out_ref[...] = jnp.concatenate([left, right], axis=1).astype(BF)


def side_by_side(at, w):
    return call(weight_kernel, "side_by_side", 8, [shaped(BF, DEEP, WIDE)], [], 0, at, w)[0]


def products(fp_ref, w_ref, c):
    left = right = None
    for z in range(N_ZL):
        w = w_ref[c * N_ZL + z]
        dims = (((0,), (0,)), ((), ()))
        one = lax.dot_general(fp_ref[z, 0], w[:, :COLS_PAD], dims, preferred_element_type=F32)
        two = lax.dot_general(fp_ref[z, 1], w[:, RIGHT:], dims, preferred_element_type=F32)
        left = one if left is None else left + one
        right = two if right is None else right + two
    return left + pltpu.roll(right, COLS_PAD - (COLS - RIGHT), axis=1)


def first_kernel(at_ref, fp_ref, w_ref, acc_ref):
    for c in range(2):
        acc_ref[c] = products(fp_ref, w_ref, c)


def second_kernel(at_ref, fp_ref, w_ref, acc_ref, img_ref, slope_ref, square_ref):
    square = jnp.zeros((1, HALF), F32)
    for c in range(2):
        v = (acc_ref[c] + products(fp_ref, w_ref, c)).T
        v = jnp.where(lax.broadcasted_iota(jnp.int32, v.shape, 0) < COLS, v, 0.0)
        v2 = v * v
        t = jnp.tanh(GELU_K * (v + GELU_C * v2 * v))
        image = (0.5 * v * (1.0 + t)).astype(BF)
        img_ref[c] = image
        slope_ref[c] = 0.5 * (1.0 + t) + 0.5 * v * (1.0 - t * t) * GELU_K * (
            1.0 + 3.0 * GELU_C * v2
        )
        m = image.astype(F32)
        square += jnp.sum(m * m, axis=0, keepdims=True)
    square_ref[...] = square


def forward(at, fp_mine, fp_other, mine, other):
    flops = HALF * TOTAL * COLS * 2
    acc = call(
        first_kernel, "first_half", 10, [shaped(F32, 2, HALF, COLS_PAD)], [], flops,
        at, fp_mine, mine,
    )[0]
    return call(
        second_kernel,
        "second_half",
        12,
        [
            shaped(BF, 2, COLS_PAD, HALF),
            shaped(F32, 2, COLS_PAD, HALF),
            shaped(F32, 1, HALF),
        ],
        [],
        flops,
        at, fp_other, other, acc,
    )


def sums_kernel(
    at_ref, img_ref, keep_ref, got_ref, gain_ref, square_ref, text_ref,
    stat_ref, cot_ref, gains_ref,
):
    zh = at_ref[0]
    terms = got_ref[COLS : COLS + 16].astype(F32)
    row = terms[0:2] + terms[2:4] + terms[4:6]
    other = jnp.concatenate(
        [jnp.broadcast_to(row[i : i + 1], (8, HALF)).T[:, :1] for i in range(2)]
    )
    gains_ref[zh] = gain_ref[...]
    gains_ref[1 - zh] = other
    rest = jnp.zeros((COLS_PAD - COLS, HALF), F32)
    cot_ref[zh, :COLS] = keep_ref[...].astype(F32) * gain_ref[:COLS]
    cot_ref[zh, COLS:] = rest
    cot_ref[1 - zh, :COLS] = got_ref[:COLS].astype(F32) * other[:COLS]
    cot_ref[1 - zh, COLS:] = rest
    cross = jnp.zeros((1, HALF), F32)
    for c in range(2):
        cross += jnp.sum(cot_ref[c] * img_ref[c].astype(F32), axis=0, keepdims=True)
    for y in range(N_Y):
        stat_ref[y, 0:1] = square_ref[...]
        stat_ref[y, 1:2] = cross
        stat_ref[y, 2:4] = text_ref[...]


def sums(zh, image, keep, got, gain, square, text):
    return call(
        sums_kernel,
        "sums",
        8,
        [
            shaped(F32, N_Y, 4, HALF),
            shaped(F32, 2, COLS_PAD, HALF),
            shaped(F32, 2, COLS_PAD, 1),
        ],
        [],
        0,
        zh, image, keep, got, gain, square, text,
    )


def backward_kernel(
    width, at_ref, slope_ref, img_ref, cot_ref, gain_ref, stat_ref, mine_ref, other_ref,
    sig_ref, conv_ref, n_ref, gp_ref, pp_ref, part_ref,
):
    stat = jnp.sum(stat_ref[:, 0:2], axis=0)
    inv = lax.rsqrt(stat[0:1] / width + EPS)
    back = inv * inv * inv * stat[1:2] / width
    for c in range(2):
        m = img_ref[c].astype(F32)
        gp = (slope_ref[c] * (inv * cot_ref[c] - back * m)).astype(BF)
        gp_ref[c, 0] = gp
        gp_ref[c, 1] = jnp.concatenate([jnp.zeros((COLS - RIGHT, HALF), BF), gp[:COLS]])
        n_ref[c] = (m * inv * gain_ref[c]).astype(BF)
    core = at_ref[0]
    for w_ref, which in ((mine_ref, core), (other_ref, 1 - core)):
        for z in range(N_ZL):
            for h, cols in ((0, slice(0, COLS_PAD)), (1, slice(RIGHT, WIDE))):
                p = jnp.dot(w_ref[z, :, cols], gp_ref[0, h], preferred_element_type=F32)
                p += jnp.dot(w_ref[N_ZL + z, :, cols], gp_ref[1, h], preferred_element_type=F32)
                pp_ref[which, z, h] = p

    def piece(begin, length):
        done = 0
        while done < length:
            owner, skip = divmod(begin + done, ROWS)
            n = min(ROWS - skip, length - done)
            c, z, x = owner % 2, owner // 2 % N_ZL, owner // (2 * N_ZL)
            row = x % 2 * ROWS + skip
            part_ref[done : done + n] = pp_ref[c, z, x // 2, row : row + n]
            done += n
        return part_ref[:length].astype(BF)

    for y in range(N_Y):
        sig_ref[y] = piece(PAIR_SIG * y, PAIR_SIG)
        conv_ref[y] = piece(PAIR_SIG * N_Y + PAIR_CONV * y, PAIR_CONV)


def backward(at, slope, image, cot, gain, stat, mine, other, width):
    return call(
        functools.partial(backward_kernel, width),
        "backward",
        22,
        [
            shaped(BF, N_Y, PAIR_SIG, HALF),
            shaped(BF, N_Y, PAIR_CONV, HALF),
            shaped(BF, 2, COLS_PAD, HALF),
        ],
        [
            pltpu.VMEM((2, 2, COLS_PAD, HALF), BF),
            pltpu.VMEM((2, N_ZL, 2, DEEP, HALF), F32),
            pltpu.VMEM((PAIR_CONV, HALF), F32),
        ],
        HALF * TOTAL * COLS * 4,
        at, slope, image, cot, gain, stat, mine, other,
    )


def per_device(sig_feat, conv_feat, weight, gain, text, grad_out, tile_count, tile_block):
    zh = lax.axis_index("zh")
    slots, tile_tokens = sig_feat.shape[:2]
    tokens = slots * tile_tokens
    model_width = COLS * N_Y * 2
    at = jnp.stack([lax.axis_index("core"), lax.axis_index("y")]).astype(jnp.int32)

    w_x = lax.all_gather(weight, ("xh", "xl"), axis=0)
    w_x, sig_feat, conv_feat = lax.optimization_barrier((w_x, sig_feat, conv_feat))
    mine = lax.all_gather(side_by_side(at, w_x), ("zh", "zl"), axis=0)

    def by_half(x):
        return jnp.stack([x[:, :HALF], x[:, HALF:]])

    xh = lax.axis_index("xh")
    sig = by_half(sig_feat.reshape(tokens, SIG).T)
    conv = by_half(conv_feat.reshape(tokens, CONV).T)
    sig = jnp.pad(sig, ((0, 0), (0, CONV - SIG), (0, 0)))
    sig, conv = exchange(
        jnp.concatenate([jnp.where(xh == 0, sig, conv), jnp.where(xh == 0, conv, sig)])
    )
    feats, right = ring_y(
        jnp.concatenate([sig.reshape(PAIR_SIG, HALF), conv.reshape(PAIR_CONV, HALF)])
    )

    live = jnp.arange(slots, dtype=jnp.int32) < tile_count[0]
    block_of = jnp.where(live, tile_block[0, :slots], -1)
    slot_block = jnp.repeat(block_of, tile_tokens)
    place = jnp.arange(tokens, dtype=jnp.int32) % tile_tokens
    seq_block = jnp.arange(tokens, dtype=jnp.int32) // tile_tokens
    chooser = (
        (slot_block[:, None] == seq_block[None, :]) & (place[:, None] == place[None, :])
    ).astype(BF)
    is_image = jnp.any(block_of[:, None] == jnp.arange(slots, dtype=jnp.int32)[None, :], axis=0)
    is_image = jnp.repeat(is_image, tile_tokens)

    def half_of(x, which):
        return lax.dynamic_slice_in_dim(x, which * HALF, HALF, 1)

    grad_slots = lax.dot_general(
        grad_out.T, chooser, (((1,), (1,)), ((), ())), preferred_element_type=F32
    ).astype(BF)
    g0 = gain.astype(BF)
    g1 = (gain - g0.astype(F32)).astype(BF)
    g2 = (gain - g0.astype(F32) - g1.astype(F32)).astype(BF)
    terms = jnp.pad(jnp.stack([g0, g1, g2]), ((0, 0), (0, COLS_PAD - COLS))).reshape(6, HALF)
    give = jnp.concatenate([half_of(grad_slots, 1 - zh), jnp.pad(terms, ((0, 10), (0, 0)))])
    keep = half_of(grad_slots, zh)

    mine, feats, right, give, keep = lax.optimization_barrier(
        (mine, feats, right, give, keep)
    )
    other = shift(mine, "core", 1)
    fp_mine, fp_other = arrange(at, feats, shift(right, "y", 1))
    got = shift(give, "zh", 1)

    image, slope, square = forward(at, fp_mine, fp_other, mine, other)
    image, slope, square, got = lax.optimization_barrier((image, slope, square, got))
    text_f = text.T.astype(F32)
    text_square = jnp.sum(text_f * text_f, axis=0).reshape(2, HALF)
    gain_own = jnp.pad(gain, (0, COLS_PAD - COLS))[:, None]
    stat, cot, gain_pair = sums(
        zh.astype(jnp.int32).reshape(1), image, keep, got, gain_own, square, text_square
    )
    stat = lax.all_to_all(stat, "y", 0, 0, tiled=True)
    sig_p, conv_p, n_image = backward(
        at, slope, image, cot, gain_pair, stat, mine, other, float(model_width)
    )
    stat, sig_p, conv_p = lax.optimization_barrier((stat, sig_p, conv_p))
    text_square = jnp.sum(stat[:, 2:], axis=0).reshape(tokens)
    conv_g = lax.psum_scatter(
        conv_p.reshape(N_Y * PAIR_CONV, HALF), "y", scatter_dimension=0, tiled=True
    ).reshape(2, CONV, HALF)
    sig_g = lax.all_to_all(sig_p, "y", 0, 0, tiled=True)
    sig_g = jnp.sum(sig_g.astype(F32), axis=0).astype(BF).reshape(2, SIG, HALF)

    def pick(x, which):
        return lax.dynamic_index_in_dim(x, which, 0, keepdims=False)

    n_image = n_image[:, :COLS]
    sig_got = shift(pick(sig_g, 1 - zh), "zh", 1)
    n_got = shift(pick(n_image, 1 - zh), "zh", 1)
    text_got = shift(text_square, "zh", 1)
    conv_g, sig_got, n_got, text_got = lax.optimization_barrier((conv_g, sig_got, n_got, text_got))

    def tokens_first(keep, got, width):
        return ordered(zh, keep, got, 1).T.reshape(slots, tile_tokens, width)

    conv_got = swap(pick(conv_g, 1 - zh), 1, 1)
    conv_keep = swap(pick(conv_g, zh), 1, 0)
    grad_conv = tokens_first(conv_keep, conv_got, CONV)
    grad_sig = tokens_first(pick(sig_g, zh), sig_got, SIG)

    n_slots = ordered(zh, pick(n_image, zh), n_got, 1)
    n_placed = jnp.dot(n_slots, chooser, preferred_element_type=F32).astype(BF)
    inv_text = lax.rsqrt((text_square + text_got) / model_width + EPS)
    n_text = (text_f * inv_text[None, :] * gain[:, None]).astype(BF)
    normed = jnp.where(is_image[None, :], n_placed, n_text).T
    return normed, grad_sig, grad_conv


def solution(mesh):
    fine = Mesh(mesh.devices.reshape(SIZES), AXES)
    dp, mp = ("xh", "xl", "zl", "core"), ("y", "zh")
    return jax.shard_map(
        per_device,
        mesh=fine,
        in_specs=(
            P(dp, None, mp),
            P(dp, None, mp),
            P(dp, mp),
            P(mp),
            P(dp, mp),
            P(dp, mp),
            P(dp),
            P(dp, None),
        ),
        out_specs=(P(dp, mp), P(dp, None, mp), P(dp, None, mp)),
        check_vma=False,
    )
```

```python
import functools

import jax
import jax.numpy as jnp
from jax import lax
from jax.experimental import pallas as pl
from jax.experimental.pallas import tpu as pltpu
from jax.sharding import Mesh
from jax.sharding import PartitionSpec as P

BF = jnp.bfloat16
F32 = jnp.float32
EPS = 1e-05
GELU_K = 0.7978845608
GELU_C = 0.044715

AXES = ("xh", "xl", "zl", "core", "y", "zh")
SIZES = (2, 2, 4, 2, 8, 2)
N_X, N_ZL, N_Y = 4, 4, 8
ROWS = 132
DEEP = 2 * ROWS
WIDE = 896
RIGHT = 384
TOTAL = 4224
COLS = 448
COLS_PAD = 512
HALF = 256
SIG = 72
CONV = 192
PAIR_SIG, PAIR_CONV = 2 * SIG, 2 * CONV
PAIR = PAIR_SIG + PAIR_CONV

VMEM = pl.BlockSpec(memory_space=pltpu.VMEM)
SMEM = pl.BlockSpec(memory_space=pltpu.SMEM)


def shift(x, axis, by):
    n = lax.axis_size(axis)
    return lax.ppermute(x, axis, [(i, (i + by) % n) for i in range(n)])


def ordered(zh, keep, got, axis):
    first = jnp.where(zh == 0, keep, got)
    second = jnp.where(zh == 0, got, keep)
    return jnp.concatenate([first, second], axis=axis)


def put(full, part, owner):
    return lax.dynamic_update_slice(full, part[None], (owner % N_Y, 0, 0))


def ring_y(block):
    me = lax.axis_index("y")
    full = put(jnp.zeros((N_Y,) + block.shape, block.dtype), block, me)
    right = left = block
    for step in range(1, N_Y // 2):
        right = shift(right, "y", 1)
        left = shift(left, "y", -1)
        full = put(full, right, me - step + N_Y)
        full = put(full, left, me + step)
    return full, right


def swap(x, dx, dz):
    pairs = [(a * 2 + b, (a + dx) % 2 * 2 + (b + dz) % 2) for a in range(2) for b in range(2)]
    return lax.ppermute(x, ("xh", "zh"), pairs)


def exchange(blocks):
    xh = lax.axis_index("xh")
    got = lax.all_to_all(blocks, ("xh", "zh"), split_axis=0, concat_axis=0, tiled=True)
    got = got.reshape((2, 2) + blocks.shape[1:])
    return (
        jnp.where(xh == 0, got[0, :, :SIG], got[1, :, :SIG]),
        jnp.where(xh == 0, got[1], got[0]),
    )


def call(kernel, name, limit, out_shape, scratch, flops, *args):
    moved = sum(x.size * x.dtype.itemsize for x in args)
    moved += sum(x.size * x.dtype.itemsize for x in out_shape)
    return pl.pallas_call(
        kernel,
        in_specs=[SMEM] + [VMEM] * (len(args) - 1),
        out_specs=[VMEM] * len(out_shape),
        out_shape=out_shape,
        scratch_shapes=scratch,
        compiler_params=pltpu.CompilerParams(vmem_limit_bytes=limit << 20),
        cost_estimate=pl.CostEstimate(flops=flops, bytes_accessed=moved, transcendentals=0),
        name=name,
    )(*args)


def shaped(dtype, *shape):
    return jax.ShapeDtypeStruct(shape, dtype)


def rows_of(x, z, c):
    return ((x * N_ZL + z) * 2 + c) * ROWS


def arrange_kernel(at_ref, feat_ref, far_ref, mine_ref, other_ref, nat_ref, part_ref):
    for y in range(N_Y):
        nat_ref[PAIR_SIG * y : PAIR_SIG * (y + 1)] = feat_ref[y, :PAIR_SIG].astype(F32)
        base = PAIR_SIG * N_Y + PAIR_CONV * y
        nat_ref[base : base + PAIR_CONV] = feat_ref[y, PAIR_SIG:].astype(F32)
    far = lax.rem(at_ref[1] + N_Y // 2, N_Y)
    row = pl.multiple_of(PAIR_SIG * far, 16)
    nat_ref[pl.ds(row, PAIR_SIG)] = far_ref[:PAIR_SIG].astype(F32)
    row = pl.multiple_of(PAIR_SIG * N_Y + PAIR_CONV * far, 16)
    nat_ref[pl.ds(row, PAIR_CONV)] = far_ref[PAIR_SIG:].astype(F32)
    for c in range(2):
        for z in range(N_ZL):
            for x in range(N_X):
                row = rows_of(x, z, c)
                part_ref[x * ROWS : (x + 1) * ROWS] = nat_ref[row : row + ROWS]
            part = part_ref[...].astype(BF).reshape(2, DEEP, HALF)

            @pl.when(at_ref[0] == c)
            def _():
                mine_ref[z] = part

            @pl.when(at_ref[0] != c)
            def _():
                other_ref[z] = part


def arrange(at, feats, far):
    return call(
        arrange_kernel,
        "arrange",
        12,
        [shaped(BF, N_ZL, 2, DEEP, HALF)] * 2,
        [pltpu.VMEM((TOTAL, HALF), F32), pltpu.VMEM((2 * DEEP, HALF), F32)],
        HALF * TOTAL * COLS * 16,
        at,
        feats,
        far,
    )


def weight_kernel(at_ref, w_ref, out_ref):
    w = w_ref[...].astype(F32)
    left = jnp.concatenate([w[0], w[1]], axis=0)
    right = jnp.concatenate([w[2], w[3]], axis=0)
    out_ref[...] = jnp.concatenate([left, right], axis=1).astype(BF)


def side_by_side(at, w):
    return call(weight_kernel, "side_by_side", 8, [shaped(BF, DEEP, WIDE)], [], 0, at, w)[0]


def products(fp_ref, w_ref, c):
    left = right = None
    for z in range(N_ZL):
        w = w_ref[c * N_ZL + z]
        dims = (((0,), (0,)), ((), ()))
        one = lax.dot_general(fp_ref[z, 0], w[:, :COLS_PAD], dims, preferred_element_type=F32)
        two = lax.dot_general(fp_ref[z, 1], w[:, RIGHT:], dims, preferred_element_type=F32)
        left = one if left is None else left + one
        right = two if right is None else right + two
    return left + pltpu.roll(right, COLS_PAD - (COLS - RIGHT), axis=1)


def first_kernel(at_ref, fp_ref, w_ref, acc_ref):
    for c in range(2):
        acc_ref[c] = products(fp_ref, w_ref, c)


def second_kernel(at_ref, fp_ref, w_ref, acc_ref, img_ref, slope_ref, square_ref):
    square = jnp.zeros((1, HALF), F32)
    for c in range(2):
        v = (acc_ref[c] + products(fp_ref, w_ref, c)).T
        v = jnp.where(lax.broadcasted_iota(jnp.int32, v.shape, 0) < COLS, v, 0.0)
        v2 = v * v
        t = jnp.tanh(GELU_K * (v + GELU_C * v2 * v))
        image = (0.5 * v * (1.0 + t)).astype(BF)
        img_ref[c] = image
        slope_ref[c] = 0.5 * (1.0 + t) + 0.5 * v * (1.0 - t * t) * GELU_K * (
            1.0 + 3.0 * GELU_C * v2
        )
        m = image.astype(F32)
        square += jnp.sum(m * m, axis=0, keepdims=True)
    square_ref[...] = square


def forward(at, fp_mine, fp_other, mine, other):
    flops = HALF * TOTAL * COLS * 8
    acc = call(
        first_kernel, "first_half", 10, [shaped(F32, 2, HALF, COLS_PAD)], [], flops,
        at, fp_mine, mine,
    )[0]
    return call(
        second_kernel,
        "second_half",
        12,
        [
            shaped(BF, 2, COLS_PAD, HALF),
            shaped(F32, 2, COLS_PAD, HALF),
            shaped(F32, 1, HALF),
        ],
        [],
        flops,
        at, fp_other, other, acc,
    )


def sums_kernel(
    at_ref, img_ref, keep_ref, got_ref, gain_ref, square_ref, text_ref,
    stat_ref, cot_ref, gains_ref,
):
    zh = at_ref[0]
    terms = got_ref[COLS : COLS + 16].astype(F32)
    row = terms[0:2] + terms[2:4] + terms[4:6]
    other = jnp.concatenate(
        [jnp.broadcast_to(row[i : i + 1], (8, HALF)).T[:, :1] for i in range(2)]
    )
    gains_ref[zh] = gain_ref[...]
    gains_ref[1 - zh] = other
    rest = jnp.zeros((COLS_PAD - COLS, HALF), F32)
    cot_ref[zh, :COLS] = keep_ref[...].astype(F32) * gain_ref[:COLS]
    cot_ref[zh, COLS:] = rest
    cot_ref[1 - zh, :COLS] = got_ref[:COLS].astype(F32) * other[:COLS]
    cot_ref[1 - zh, COLS:] = rest
    cross = jnp.zeros((1, HALF), F32)
    for c in range(2):
        cross += jnp.sum(cot_ref[c] * img_ref[c].astype(F32), axis=0, keepdims=True)
    for y in range(N_Y):
        stat_ref[y, 0:1] = square_ref[...]
        stat_ref[y, 1:2] = cross
        stat_ref[y, 2:4] = text_ref[...]


def sums(zh, image, keep, got, gain, square, text):
    return call(
        sums_kernel,
        "sums",
        8,
        [
            shaped(F32, N_Y, 4, HALF),
            shaped(F32, 2, COLS_PAD, HALF),
            shaped(F32, 2, COLS_PAD, 1),
        ],
        [],
        0,
        zh, image, keep, got, gain, square, text,
    )


def backward_kernel(
    width, at_ref, slope_ref, img_ref, cot_ref, gain_ref, stat_ref, mine_ref, other_ref,
    sig_ref, conv_ref, n_ref, gp_ref, pp_ref, part_ref,
):
    stat = jnp.sum(stat_ref[:, 0:2], axis=0)
    inv = lax.rsqrt(stat[0:1] / width + EPS)
    back = inv * inv * inv * stat[1:2] / width
    for c in range(2):
        m = img_ref[c].astype(F32)
        gp = (slope_ref[c] * (inv * cot_ref[c] - back * m)).astype(BF)
        gp_ref[c, 0] = gp
        gp_ref[c, 1] = jnp.concatenate([jnp.zeros((COLS - RIGHT, HALF), BF), gp[:COLS]])
        n_ref[c] = (m * inv * gain_ref[c]).astype(BF)
    core = at_ref[0]
    for w_ref, which in ((mine_ref, core), (other_ref, 1 - core)):
        for z in range(N_ZL):
            for h, cols in ((0, slice(0, COLS_PAD)), (1, slice(RIGHT, WIDE))):
                p = jnp.dot(w_ref[z, :, cols], gp_ref[0, h], preferred_element_type=F32)
                p += jnp.dot(w_ref[N_ZL + z, :, cols], gp_ref[1, h], preferred_element_type=F32)
                pp_ref[which, z, h] = p

    def piece(begin, length):
        done = 0
        while done < length:
            owner, skip = divmod(begin + done, ROWS)
            n = min(ROWS - skip, length - done)
            c, z, x = owner % 2, owner // 2 % N_ZL, owner // (2 * N_ZL)
            row = x % 2 * ROWS + skip
            part_ref[done : done + n] = pp_ref[c, z, x // 2, row : row + n]
            done += n
        return part_ref[:length].astype(BF)

    for y in range(N_Y):
        sig_ref[y] = piece(PAIR_SIG * y, PAIR_SIG)
        conv_ref[y] = piece(PAIR_SIG * N_Y + PAIR_CONV * y, PAIR_CONV)


def backward(at, slope, image, cot, gain, stat, mine, other, width):
    return call(
        functools.partial(backward_kernel, width),
        "backward",
        22,
        [
            shaped(BF, N_Y, PAIR_SIG, HALF),
            shaped(BF, N_Y, PAIR_CONV, HALF),
            shaped(BF, 2, COLS_PAD, HALF),
        ],
        [
            pltpu.VMEM((2, 2, COLS_PAD, HALF), BF),
            pltpu.VMEM((2, N_ZL, 2, DEEP, HALF), F32),
            pltpu.VMEM((PAIR_CONV, HALF), F32),
        ],
        HALF * TOTAL * COLS * 4,
        at, slope, image, cot, gain, stat, mine, other,
    )


def per_device(sig_feat, conv_feat, weight, gain, text, grad_out, tile_count, tile_block):
    zh = lax.axis_index("zh")
    slots, tile_tokens = sig_feat.shape[:2]
    tokens = slots * tile_tokens
    model_width = COLS * N_Y * 2
    at = jnp.stack([lax.axis_index("core"), lax.axis_index("y")]).astype(jnp.int32)

    w_x = lax.all_gather(weight, ("xh", "xl"), axis=0)
    w_x, sig_feat, conv_feat = lax.optimization_barrier((w_x, sig_feat, conv_feat))
    mine = lax.all_gather(side_by_side(at, w_x), ("zh", "zl"), axis=0)

    def by_half(x):
        return jnp.stack([x[:, :HALF], x[:, HALF:]])

    xh = lax.axis_index("xh")
    sig = by_half(sig_feat.reshape(tokens, SIG).T)
    conv = by_half(conv_feat.reshape(tokens, CONV).T)
    sig = jnp.pad(sig, ((0, 0), (0, CONV - SIG), (0, 0)))
    sig, conv = exchange(
        jnp.concatenate([jnp.where(xh == 0, sig, conv), jnp.where(xh == 0, conv, sig)])
    )
    feats, right = ring_y(
        jnp.concatenate([sig.reshape(PAIR_SIG, HALF), conv.reshape(PAIR_CONV, HALF)])
    )

    live = jnp.arange(slots, dtype=jnp.int32) < tile_count[0]
    block_of = jnp.where(live, tile_block[0, :slots], -1)
    slot_block = jnp.repeat(block_of, tile_tokens)
    place = jnp.arange(tokens, dtype=jnp.int32) % tile_tokens
    seq_block = jnp.arange(tokens, dtype=jnp.int32) // tile_tokens
    chooser = (
        (slot_block[:, None] == seq_block[None, :]) & (place[:, None] == place[None, :])
    ).astype(BF)
    is_image = jnp.any(block_of[:, None] == jnp.arange(slots, dtype=jnp.int32)[None, :], axis=0)
    is_image = jnp.repeat(is_image, tile_tokens)

    def half_of(x, which):
        return lax.dynamic_slice_in_dim(x, which * HALF, HALF, 1)

    grad_slots = lax.dot_general(
        grad_out.T, chooser, (((1,), (1,)), ((), ())), preferred_element_type=F32
    ).astype(BF)
    g0 = gain.astype(BF)
    g1 = (gain - g0.astype(F32)).astype(BF)
    g2 = (gain - g0.astype(F32) - g1.astype(F32)).astype(BF)
    terms = jnp.pad(jnp.stack([g0, g1, g2]), ((0, 0), (0, COLS_PAD - COLS))).reshape(6, HALF)
    give = jnp.concatenate([half_of(grad_slots, 1 - zh), jnp.pad(terms, ((0, 10), (0, 0)))])
    keep = half_of(grad_slots, zh)

    mine, feats, right, give, keep = lax.optimization_barrier(
        (mine, feats, right, give, keep)
    )
    other = shift(mine, "core", 1)
    fp_mine, fp_other = arrange(at, feats, shift(right, "y", 1))
    got = shift(give, "zh", 1)

    image, slope, square = forward(at, fp_mine, fp_other, mine, other)
    image, slope, square, got = lax.optimization_barrier((image, slope, square, got))
    text_f = text.T.astype(F32)
    text_square = jnp.sum(text_f * text_f, axis=0).reshape(2, HALF)
    gain_own = jnp.pad(gain, (0, COLS_PAD - COLS))[:, None]
    stat, cot, gain_pair = sums(
        zh.astype(jnp.int32).reshape(1), image, keep, got, gain_own, square, text_square
    )
    stat = lax.all_to_all(stat, "y", 0, 0, tiled=True)
    sig_p, conv_p, n_image = backward(
        at, slope, image, cot, gain_pair, stat, mine, other, float(model_width)
    )
    stat, sig_p, conv_p = lax.optimization_barrier((stat, sig_p, conv_p))
    text_square = jnp.sum(stat[:, 2:], axis=0).reshape(tokens)
    conv_g = lax.psum_scatter(
        conv_p.reshape(N_Y * PAIR_CONV, HALF), "y", scatter_dimension=0, tiled=True
    ).reshape(2, CONV, HALF)
    sig_g = lax.all_to_all(sig_p, "y", 0, 0, tiled=True)
    sig_g = jnp.sum(sig_g.astype(F32), axis=0).astype(BF).reshape(2, SIG, HALF)

    def pick(x, which):
        return lax.dynamic_index_in_dim(x, which, 0, keepdims=False)

    n_image = n_image[:, :COLS]
    sig_got = shift(pick(sig_g, 1 - zh), "zh", 1)
    n_got = shift(pick(n_image, 1 - zh), "zh", 1)
    text_got = shift(text_square, "zh", 1)
    conv_g, sig_got, n_got, text_got = lax.optimization_barrier((conv_g, sig_got, n_got, text_got))

    def tokens_first(keep, got, width):
        return ordered(zh, keep, got, 1).T.reshape(slots, tile_tokens, width)

    conv_got = swap(pick(conv_g, 1 - zh), 1, 1)
    conv_keep = swap(pick(conv_g, zh), 1, 0)
    grad_conv = tokens_first(conv_keep, conv_got, CONV)
    grad_sig = tokens_first(pick(sig_g, zh), sig_got, SIG)

    n_slots = ordered(zh, pick(n_image, zh), n_got, 1)
    n_placed = jnp.dot(n_slots, chooser, preferred_element_type=F32).astype(BF)
    inv_text = lax.rsqrt((text_square + text_got) / model_width + EPS)
    n_text = (text_f * inv_text[None, :] * gain[:, None]).astype(BF)
    normed = jnp.where(is_image[None, :], n_placed, n_text).T
    return normed, grad_sig, grad_conv


def solution(mesh):
    fine = Mesh(mesh.devices.reshape(SIZES), AXES)
    dp, mp = ("xh", "xl", "zl", "core"), ("y", "zh")
    return jax.shard_map(
        per_device,
        mesh=fine,
        in_specs=(
            P(dp, None, mp),
            P(dp, None, mp),
            P(dp, mp),
            P(mp),
            P(dp, mp),
            P(dp, mp),
            P(dp),
            P(dp, None),
        ),
        out_specs=(P(dp, mp), P(dp, None, mp), P(dp, None, mp)),
        check_vma=False,
    )
```

```python
import functools

import jax
import jax.numpy as jnp
from jax import lax
from jax.experimental import pallas as pl
from jax.experimental.pallas import tpu as pltpu
from jax.sharding import Mesh
from jax.sharding import PartitionSpec as P

BF = jnp.bfloat16
F32 = jnp.float32
EPS = 1e-05
GELU_K = 0.7978845608
GELU_C = 0.044715

AXES = ("xh", "xl", "zl", "core", "y", "zh")
SIZES = (2, 2, 4, 2, 8, 2)
N_X, N_ZL, N_Y = 4, 4, 8
ROWS = 132
DEEP = 2 * ROWS
WIDE = 896
RIGHT = 384
TOTAL = 4224
COLS = 448
COLS_PAD = 512
HALF = 256
SIG = 72
CONV = 192
PAIR_SIG, PAIR_CONV = 2 * SIG, 2 * CONV
PAIR = PAIR_SIG + PAIR_CONV

VMEM = pl.BlockSpec(memory_space=pltpu.VMEM)
SMEM = pl.BlockSpec(memory_space=pltpu.SMEM)


def shift(x, axis, by):
    n = lax.axis_size(axis)
    return lax.ppermute(x, axis, [(i, (i + by) % n) for i in range(n)])


def ordered(zh, keep, got, axis):
    first = jnp.where(zh == 0, keep, got)
    second = jnp.where(zh == 0, got, keep)
    return jnp.concatenate([first, second], axis=axis)


def put(full, part, owner):
    return lax.dynamic_update_slice(full, part[None], (owner % N_Y, 0, 0))


def ring_y(block):
    me = lax.axis_index("y")
    full = put(jnp.zeros((N_Y,) + block.shape, block.dtype), block, me)
    right = left = block
    for step in range(1, N_Y // 2):
        right = shift(right, "y", 1)
        left = shift(left, "y", -1)
        full = put(full, right, me - step + N_Y)
        full = put(full, left, me + step)
    return full, right


def swap(x, dx, dz):
    pairs = [(a * 2 + b, (a + dx) % 2 * 2 + (b + dz) % 2) for a in range(2) for b in range(2)]
    return lax.ppermute(x, ("xh", "zh"), pairs)


def exchange(blocks):
    xh = lax.axis_index("xh")
    got = lax.all_to_all(blocks, ("xh", "zh"), split_axis=0, concat_axis=0, tiled=True)
    got = got.reshape((2, 2) + blocks.shape[1:])
    return (
        jnp.where(xh == 0, got[0, :, :SIG], got[1, :, :SIG]),
        jnp.where(xh == 0, got[1], got[0]),
    )


def call(kernel, name, limit, out_shape, scratch, flops, *args):
    moved = sum(x.size * x.dtype.itemsize for x in args)
    moved += sum(x.size * x.dtype.itemsize for x in out_shape)
    return pl.pallas_call(
        kernel,
        in_specs=[SMEM] + [VMEM] * (len(args) - 1),
        out_specs=[VMEM] * len(out_shape),
        out_shape=out_shape,
        scratch_shapes=scratch,
        compiler_params=pltpu.CompilerParams(vmem_limit_bytes=limit << 20),
        cost_estimate=pl.CostEstimate(flops=flops, bytes_accessed=moved, transcendentals=0),
        name=name,
    )(*args)


def shaped(dtype, *shape):
    return jax.ShapeDtypeStruct(shape, dtype)


def rows_of(x, z, c):
    return ((x * N_ZL + z) * 2 + c) * ROWS


def arrange_kernel(at_ref, feat_ref, far_ref, mine_ref, other_ref, nat_ref, part_ref):
    for y in range(N_Y):
        nat_ref[PAIR_SIG * y : PAIR_SIG * (y + 1)] = feat_ref[y, :PAIR_SIG].astype(F32)
        base = PAIR_SIG * N_Y + PAIR_CONV * y
        nat_ref[base : base + PAIR_CONV] = feat_ref[y, PAIR_SIG:].astype(F32)
    far = lax.rem(at_ref[1] + N_Y // 2, N_Y)
    row = pl.multiple_of(PAIR_SIG * far, 16)
    nat_ref[pl.ds(row, PAIR_SIG)] = far_ref[:PAIR_SIG].astype(F32)
    row = pl.multiple_of(PAIR_SIG * N_Y + PAIR_CONV * far, 16)
    nat_ref[pl.ds(row, PAIR_CONV)] = far_ref[PAIR_SIG:].astype(F32)
    for c in range(2):
        for z in range(N_ZL):
            for x in range(N_X):
                row = rows_of(x, z, c)
                part_ref[x * ROWS : (x + 1) * ROWS] = nat_ref[row : row + ROWS]
            part = part_ref[...].astype(BF).reshape(2, DEEP, HALF)

            @pl.when(at_ref[0] == c)
            def _():
                mine_ref[z] = part

            @pl.when(at_ref[0] != c)
            def _():
                other_ref[z] = part


def arrange(at, feats, far):
    return call(
        arrange_kernel,
        "arrange",
        12,
        [shaped(BF, N_ZL, 2, DEEP, HALF)] * 2,
        [pltpu.VMEM((TOTAL, HALF), F32), pltpu.VMEM((2 * DEEP, HALF), F32)],
        HALF * TOTAL * COLS * 16,
        at,
        feats,
        far,
    )


def weight_kernel(at_ref, w_ref, out_ref):
    w = w_ref[...].astype(F32)
    left = jnp.concatenate([w[0], w[1]], axis=0)
    right = jnp.concatenate([w[2], w[3]], axis=0)
    out_ref[...] = jnp.concatenate([left, right], axis=1).astype(BF)


def side_by_side(at, w):
    return call(weight_kernel, "side_by_side", 8, [shaped(BF, DEEP, WIDE)], [], 0, at, w)[0]


def products(fp_ref, w_ref, c):
    left = right = None
    for z in range(N_ZL):
        w = w_ref[c * N_ZL + z]
        dims = (((0,), (0,)), ((), ()))
        one = lax.dot_general(fp_ref[z, 0], w[:, :COLS_PAD], dims, preferred_element_type=F32)
        two = lax.dot_general(fp_ref[z, 1], w[:, RIGHT:], dims, preferred_element_type=F32)
        left = one if left is None else left + one
        right = two if right is None else right + two
    return left + pltpu.roll(right, COLS_PAD - (COLS - RIGHT), axis=1)


def first_kernel(at_ref, fp_ref, w_ref, acc_ref):
    for c in range(2):
        acc_ref[c] = products(fp_ref, w_ref, c)


def second_kernel(at_ref, fp_ref, w_ref, acc_ref, img_ref, slope_ref, square_ref):
    square = jnp.zeros((1, HALF), F32)
    for c in range(2):
        v = (acc_ref[c] + products(fp_ref, w_ref, c)).T
        v = jnp.where(lax.broadcasted_iota(jnp.int32, v.shape, 0) < COLS, v, 0.0)
        v2 = v * v
        t = jnp.tanh(GELU_K * (v + GELU_C * v2 * v))
        image = (0.5 * v * (1.0 + t)).astype(BF)
        img_ref[c] = image
        slope_ref[c] = 0.5 * (1.0 + t) + 0.5 * v * (1.0 - t * t) * GELU_K * (
            1.0 + 3.0 * GELU_C * v2
        )
        m = image.astype(F32)
        square += jnp.sum(m * m, axis=0, keepdims=True)
    square_ref[...] = square


def forward(at, fp_mine, fp_other, mine, other):
    flops = HALF * TOTAL * COLS * 8
    acc = call(
        first_kernel, "first_half", 10, [shaped(F32, 2, HALF, COLS_PAD)], [], flops,
        at, fp_mine, mine,
    )[0]
    return call(
        second_kernel,
        "second_half",
        12,
        [
            shaped(BF, 2, COLS_PAD, HALF),
            shaped(F32, 2, COLS_PAD, HALF),
            shaped(F32, 1, HALF),
        ],
        [],
        flops,
        at, fp_other, other, acc,
    )


def sums_kernel(
    at_ref, img_ref, keep_ref, got_ref, gain_ref, square_ref, text_ref,
    stat_ref, cot_ref, gains_ref,
):
    zh = at_ref[0]
    terms = got_ref[COLS : COLS + 16].astype(F32)
    row = terms[0:2] + terms[2:4] + terms[4:6]
    other = jnp.concatenate(
        [jnp.broadcast_to(row[i : i + 1], (8, HALF)).T[:, :1] for i in range(2)]
    )
    gains_ref[zh] = gain_ref[...]
    gains_ref[1 - zh] = other
    rest = jnp.zeros((COLS_PAD - COLS, HALF), F32)
    cot_ref[zh, :COLS] = keep_ref[...].astype(F32) * gain_ref[:COLS]
    cot_ref[zh, COLS:] = rest
    cot_ref[1 - zh, :COLS] = got_ref[:COLS].astype(F32) * other[:COLS]
    cot_ref[1 - zh, COLS:] = rest
    cross = jnp.zeros((1, HALF), F32)
    for c in range(2):
        cross += jnp.sum(cot_ref[c] * img_ref[c].astype(F32), axis=0, keepdims=True)
    for y in range(N_Y):
        stat_ref[y, 0:1] = square_ref[...]
        stat_ref[y, 1:2] = cross
        stat_ref[y, 2:4] = text_ref[...]


def sums(zh, image, keep, got, gain, square, text):
    return call(
        sums_kernel,
        "sums",
        8,
        [
            shaped(F32, N_Y, 4, HALF),
            shaped(F32, 2, COLS_PAD, HALF),
            shaped(F32, 2, COLS_PAD, 1),
        ],
        [],
        0,
        zh, image, keep, got, gain, square, text,
    )


def backward_kernel(
    width, at_ref, slope_ref, img_ref, cot_ref, gain_ref, stat_ref, mine_ref, other_ref,
    sig_ref, conv_ref, n_ref, gp_ref, pp_ref, part_ref,
):
    stat = jnp.sum(stat_ref[:, 0:2], axis=0)
    inv = lax.rsqrt(stat[0:1] / width + EPS)
    back = inv * inv * inv * stat[1:2] / width
    for c in range(2):
        m = img_ref[c].astype(F32)
        gp = (slope_ref[c] * (inv * cot_ref[c] - back * m)).astype(BF)
        gp_ref[c, 0] = gp
        gp_ref[c, 1] = jnp.concatenate([jnp.zeros((COLS - RIGHT, HALF), BF), gp[:COLS]])
        n_ref[c] = (m * inv * gain_ref[c]).astype(BF)
    core = at_ref[0]
    for w_ref, which in ((mine_ref, core), (other_ref, 1 - core)):
        for z in range(N_ZL):
            for h, cols in ((0, slice(0, COLS_PAD)), (1, slice(RIGHT, WIDE))):
                p = jnp.dot(w_ref[z, :, cols], gp_ref[0, h], preferred_element_type=F32)
                p += jnp.dot(w_ref[N_ZL + z, :, cols], gp_ref[1, h], preferred_element_type=F32)
                pp_ref[which, z, h] = p

    def piece(begin, length):
        done = 0
        while done < length:
            owner, skip = divmod(begin + done, ROWS)
            n = min(ROWS - skip, length - done)
            c, z, x = owner % 2, owner // 2 % N_ZL, owner // (2 * N_ZL)
            row = x % 2 * ROWS + skip
            part_ref[done : done + n] = pp_ref[c, z, x // 2, row : row + n]
            done += n
        return part_ref[:length].astype(BF)

    for y in range(N_Y):
        sig_ref[y] = piece(PAIR_SIG * y, PAIR_SIG)
        conv_ref[y] = piece(PAIR_SIG * N_Y + PAIR_CONV * y, PAIR_CONV)


def backward(at, slope, image, cot, gain, stat, mine, other, width):
    return call(
        functools.partial(backward_kernel, width),
        "backward",
        22,
        [
            shaped(BF, N_Y, PAIR_SIG, HALF),
            shaped(BF, N_Y, PAIR_CONV, HALF),
            shaped(BF, 2, COLS_PAD, HALF),
        ],
        [
            pltpu.VMEM((2, 2, COLS_PAD, HALF), BF),
            pltpu.VMEM((2, N_ZL, 2, DEEP, HALF), F32),
            pltpu.VMEM((PAIR_CONV, HALF), F32),
        ],
        HALF * TOTAL * COLS * 4,
        at, slope, image, cot, gain, stat, mine, other,
    )


def per_device(sig_feat, conv_feat, weight, gain, text, grad_out, tile_count, tile_block):
    zh = lax.axis_index("zh")
    slots, tile_tokens = sig_feat.shape[:2]
    tokens = slots * tile_tokens
    model_width = COLS * N_Y * 2
    at = jnp.stack([lax.axis_index("core"), lax.axis_index("y")]).astype(jnp.int32)

    w_x = lax.all_gather(weight, ("xh", "xl"), axis=0)
    w_x, sig_feat, conv_feat = lax.optimization_barrier((w_x, sig_feat, conv_feat))
    mine = lax.all_gather(side_by_side(at, w_x), ("zh", "zl"), axis=0)

    def by_half(x):
        return jnp.stack([x[:, :HALF], x[:, HALF:]])

    xh = lax.axis_index("xh")
    sig = by_half(sig_feat.reshape(tokens, SIG).T)
    conv = by_half(conv_feat.reshape(tokens, CONV).T)
    sig = jnp.pad(sig, ((0, 0), (0, CONV - SIG), (0, 0)))
    sig, conv = exchange(
        jnp.concatenate([jnp.where(xh == 0, sig, conv), jnp.where(xh == 0, conv, sig)])
    )
    feats, right = ring_y(
        jnp.concatenate([sig.reshape(PAIR_SIG, HALF), conv.reshape(PAIR_CONV, HALF)])
    )

    live = jnp.arange(slots, dtype=jnp.int32) < tile_count[0]
    block_of = jnp.where(live, tile_block[0, :slots], -1)
    slot_block = jnp.repeat(block_of, tile_tokens)
    place = jnp.arange(tokens, dtype=jnp.int32) % tile_tokens
    seq_block = jnp.arange(tokens, dtype=jnp.int32) // tile_tokens
    chooser = (
        (slot_block[:, None] == seq_block[None, :]) & (place[:, None] == place[None, :])
    ).astype(BF)
    is_image = jnp.any(block_of[:, None] == jnp.arange(slots, dtype=jnp.int32)[None, :], axis=0)
    is_image = jnp.repeat(is_image, tile_tokens)

    def half_of(x, which):
        return lax.dynamic_slice_in_dim(x, which * HALF, HALF, 1)

    grad_slots = lax.dot_general(
        grad_out.T, chooser, (((1,), (1,)), ((), ())), preferred_element_type=F32
    ).astype(BF)
    g0 = gain.astype(BF)
    g1 = (gain - g0.astype(F32)).astype(BF)
    g2 = (gain - g0.astype(F32) - g1.astype(F32)).astype(BF)
    terms = jnp.pad(jnp.stack([g0, g1, g2]), ((0, 0), (0, COLS_PAD - COLS))).reshape(6, HALF)
    give = jnp.concatenate([half_of(grad_slots, 1 - zh), jnp.pad(terms, ((0, 10), (0, 0)))])
    keep = half_of(grad_slots, zh)

    mine, _, _, give, keep = lax.optimization_barrier((mine, feats, right, give, keep))
    other = shift(mine, "core", 1)
    fp_mine, fp_other = arrange(at, feats, shift(right, "y", 1))
    got = shift(give, "zh", 1)

    image, slope, square = forward(at, fp_mine, fp_other, mine, other)
    image, slope, square, got = lax.optimization_barrier((image, slope, square, got))
    text_f = text.T.astype(F32)
    text_square = jnp.sum(text_f * text_f, axis=0).reshape(2, HALF)
    gain_own = jnp.pad(gain, (0, COLS_PAD - COLS))[:, None]
    stat, cot, gain_pair = sums(
        zh.astype(jnp.int32).reshape(1), image, keep, got, gain_own, square, text_square
    )
    stat = lax.all_to_all(stat, "y", 0, 0, tiled=True)
    sig_p, conv_p, n_image = backward(
        at, slope, image, cot, gain_pair, stat, mine, other, float(model_width)
    )
    stat, sig_p, conv_p = lax.optimization_barrier((stat, sig_p, conv_p))
    text_square = jnp.sum(stat[:, 2:], axis=0).reshape(tokens)
    conv_g = lax.psum_scatter(
        conv_p.reshape(N_Y * PAIR_CONV, HALF), "y", scatter_dimension=0, tiled=True
    ).reshape(2, CONV, HALF)
    sig_g = lax.all_to_all(sig_p, "y", 0, 0, tiled=True)
    sig_g = jnp.sum(sig_g.astype(F32), axis=0).astype(BF).reshape(2, SIG, HALF)

    def pick(x, which):
        return lax.dynamic_index_in_dim(x, which, 0, keepdims=False)

    n_image = n_image[:, :COLS]
    sig_got = shift(pick(sig_g, 1 - zh), "zh", 1)
    n_got = shift(pick(n_image, 1 - zh), "zh", 1)
    text_got = shift(text_square, "zh", 1)
    conv_g, sig_got, n_got, text_got = lax.optimization_barrier((conv_g, sig_got, n_got, text_got))

    def tokens_first(keep, got, width):
        return ordered(zh, keep, got, 1).T.reshape(slots, tile_tokens, width)

    conv_got = swap(pick(conv_g, 1 - zh), 1, 1)
    conv_keep = swap(pick(conv_g, zh), 1, 0)
    grad_conv = tokens_first(conv_keep, conv_got, CONV)
    grad_sig = tokens_first(pick(sig_g, zh), sig_got, SIG)

    n_slots = ordered(zh, pick(n_image, zh), n_got, 1)
    n_placed = jnp.dot(n_slots, chooser, preferred_element_type=F32).astype(BF)
    inv_text = lax.rsqrt((text_square + text_got) / model_width + EPS)
    n_text = (text_f * inv_text[None, :] * gain[:, None]).astype(BF)
    normed = jnp.where(is_image[None, :], n_placed, n_text).T
    return normed, grad_sig, grad_conv


def solution(mesh):
    fine = Mesh(mesh.devices.reshape(SIZES), AXES)
    dp, mp = ("xh", "xl", "zl", "core"), ("y", "zh")
    return jax.shard_map(
        per_device,
        mesh=fine,
        in_specs=(
            P(dp, None, mp),
            P(dp, None, mp),
            P(dp, mp),
            P(mp),
            P(dp, mp),
            P(dp, mp),
            P(dp),
            P(dp, None),
        ),
        out_specs=(P(dp, mp), P(dp, None, mp), P(dp, None, mp)),
        check_vma=False,
    )
```
